32 devices in a mesh: wide: 16 (over z, y, x), narrow: 2 (over core).
Axes of the slice: x: 2, y: 2, z: 4, core: 2. Of those that a mesh axis runs over, the one named last changes fastest.
Arguments:
- load: float32 [2048, 512], P(('wide', 'narrow')), may hold values from -48 to 48
- geom: bfloat16 [7, 2048, 512], P(None, ('wide', 'narrow')), may hold values from -0.15 to 3, as said below
- element_order: int32 [16, 2, 64], P('wide', 'narrow'), may hold values from 0 to 63, each once within a row
Outputs:
- solution: float32 [2048, 512], P(('wide', 'narrow'))
- residual: float32 [2048, 512], P(('wide', 'narrow'))
The draws below stay inside these ranges and needn't reach their ends.
Inputs may be any that keep to these rules, and one draw needn't show every extreme that they name: `geom`: at every point G0, G1, G2 and G6 are positive and |G3|, |G4|, |G5| stay below 0.15. `element_order`: each device's list names each of its 64 block positions exactly once.
All inputs are finite; a program needn't handle non-finite values.
Results may differ from the reference program's by a relative error of at most 0.02.
Values sent between devices are 32-bit elements; how exact they have to be, the bound alone decides.
A program may use at most 64 MiB of HBM per device.

```python
import math
import jax
import jax.numpy as jnp
import numpy as np
from jax import lax

EZ = 1
EA = 4
ER = 16
CHEB = 3
ITERS = 2
E_DEV = 64
ELEMS = 2048
N_WIDE = 16
N_NARROW = 2


def draw_load(key, part):
    key = jax.random.fold_in(key, 11)
    device = jnp.arange(ELEMS, dtype=jnp.int32) // E_DEV
    wide_index = device // N_NARROW
    narrow_index = device % N_NARROW
    smooth_wide = jax.random.uniform(jax.random.fold_in(key, 4), (N_WIDE,), jnp.float32, minval=0.0, maxval=math.log(4.0))
    smooth_narrow = jax.random.uniform(jax.random.fold_in(key, 5), (N_NARROW,), jnp.float32, minval=0.0, maxval=math.log(4.0))
    rough_wide = jax.random.uniform(jax.random.fold_in(key, 6), (N_WIDE,), jnp.float32, minval=0.0, maxval=math.log(2.0))
    rough_narrow = jax.random.uniform(jax.random.fold_in(key, 7), (N_NARROW,), jnp.float32, minval=0.0, maxval=math.log(2.0))
    rise = 1.0 + 2.0 * wide_index.astype(jnp.float32) / max(N_WIDE - 1, 1)
    smooth_level = 0.4 * jnp.exp(smooth_wide[wide_index] + smooth_narrow[narrow_index])
    rough_level = 0.5 * jnp.exp(rough_wide[wide_index] + rough_narrow[narrow_index]) * rise
    point = jnp.arange(512, dtype=jnp.int32)
    node_i = point // 64
    node_j = point // 8 % 8
    node_k = point % 8
    half_i = jnp.where((node_i == 0) | (node_i == 7), 0.5, 1.0)
    half_j = jnp.where((node_j == 0) | (node_j == 7), 0.5, 1.0)
    half_k = jnp.where((node_k == 0) | (node_k == 7), 0.5, 1.0)
    pattern = (half_i * half_j * half_k).astype(jnp.float32)
    smooth = smooth_level[:, None] * pattern[None, :]
    rough = jnp.clip(jax.random.normal(jax.random.fold_in(key, 3), (ELEMS, 512), jnp.float32), -6.0, 6.0)
    return (smooth + rough_level[:, None] * rough).astype(jnp.float32)


def draw_geom(key, part):
    key = jax.random.fold_in(key, 23)
    shape = (ELEMS, 512)
    diagonal = jnp.exp(jax.random.uniform(jax.random.fold_in(key, 2), (3,) + shape, jnp.float32, minval=math.log(0.5), maxval=math.log(2.0)))
    cross = jax.random.uniform(jax.random.fold_in(key, 3), (3,) + shape, jnp.float32, minval=-0.14, maxval=0.14)
    screen = jnp.exp(jax.random.uniform(jax.random.fold_in(key, 4), (1,) + shape, jnp.float32, minval=math.log(0.25), maxval=math.log(2.5)))
    return jnp.concatenate([diagonal, cross, screen], axis=0).astype(jnp.bfloat16)


def setup_inputs(seed: int = 0) -> dict:
    key_list = jax.random.split(jax.random.key(seed), 4)
    return {
        "load": draw_load(jax.random.fold_in(key_list[3], 71), 0),
        "geom": draw_geom(jax.random.fold_in(key_list[3], 71), 0),
        "element_order": jax.vmap(lambda own: jax.random.permutation(own, E_DEV))(jax.random.split(key_list[2], N_WIDE * N_NARROW)).reshape((N_WIDE, N_NARROW, E_DEV)).astype(jnp.int32),
    }


interval_low = 0.03
interval_high = 1.0


def legendre_seven(point):
    before = 1.0
    current = point
    for degree in range(1, 7):
        after = ((2.0 * degree + 1.0) * point * current - degree * before) / (degree + 1.0)
        before = current
        current = after
    return current


def gll_derivative():
    points = 8
    inner_nodes = [-0.8717401485096066, -0.5917001814331423, -0.2092992179024789, 0.2092992179024789, 0.5917001814331423, 0.8717401485096066]
    nodes = [-1.0] + inner_nodes + [1.0]
    values_at = [legendre_seven(node) for node in nodes]
    matrix = np.zeros((points, points))
    for source in range(points):
        for target in range(points):
            if source != target:
                matrix[source, target] = values_at[source] / (values_at[target] * (nodes[source] - nodes[target]))
    matrix[0, 0] = -(points - 1) * points / 4.0
    matrix[points - 1, points - 1] = (points - 1) * points / 4.0
    return matrix


def gradients(field, derivative):
    pipe_len, cycle_len, radial_len = field.shape
    blocks = field.reshape(pipe_len // 8, 8, cycle_len // 8, 8, radial_len // 8, 8)
    highest = lax.Precision.HIGHEST
    grad_z = jnp.einsum("im,pmqjsk->piqjsk", derivative, blocks, precision=highest)
    grad_a = jnp.einsum("jm,piqmsk->piqjsk", derivative, blocks, precision=highest)
    grad_r = jnp.einsum("km,piqjsm->piqjsk", derivative, blocks, precision=highest)
    return grad_z.reshape(field.shape), grad_a.reshape(field.shape), grad_r.reshape(field.shape)


def divergence(flux_z, flux_a, flux_r, derivative):
    pipe_len, cycle_len, radial_len = flux_z.shape
    shape6 = (pipe_len // 8, 8, cycle_len // 8, 8, radial_len // 8, 8)
    highest = lax.Precision.HIGHEST
    part_z = jnp.einsum("mi,pmqjsk->piqjsk", derivative, flux_z.reshape(shape6), precision=highest)
    part_a = jnp.einsum("mj,piqmsk->piqjsk", derivative, flux_a.reshape(shape6), precision=highest)
    part_r = jnp.einsum("mk,piqjsm->piqjsk", derivative, flux_r.reshape(shape6), precision=highest)
    return (part_z + part_a + part_r).reshape(flux_z.shape)


def element_apply(field, metric, derivative):
    grad_z, grad_a, grad_r = gradients(field, derivative)
    g_zz = metric[0].astype(jnp.float32)
    g_aa = metric[1].astype(jnp.float32)
    g_rr = metric[2].astype(jnp.float32)
    g_za = metric[3].astype(jnp.float32)
    g_zr = metric[4].astype(jnp.float32)
    g_ar = metric[5].astype(jnp.float32)
    flux_z = g_zz * grad_z + g_za * grad_a + g_zr * grad_r
    flux_a = g_za * grad_z + g_aa * grad_a + g_ar * grad_r
    flux_r = g_zr * grad_z + g_ar * grad_a + g_rr * grad_r
    return divergence(flux_z, flux_a, flux_r, derivative) + metric[6].astype(jnp.float32) * field


def element_bound(metric, derivative):
    pipe_len, cycle_len, radial_len = metric.shape[1:]
    absolute = jnp.abs(derivative)
    row_total = jnp.sum(absolute, axis=1)
    q_z = jnp.tile(row_total, pipe_len // 8)[:, None, None]
    q_a = jnp.tile(row_total, cycle_len // 8)[None, :, None]
    q_r = jnp.tile(row_total, radial_len // 8)[None, None, :]
    g_abs = jnp.abs(metric.astype(jnp.float32))
    h_z = g_abs[0] * q_z + g_abs[3] * q_a + g_abs[4] * q_r
    h_a = g_abs[3] * q_z + g_abs[1] * q_a + g_abs[5] * q_r
    h_r = g_abs[4] * q_z + g_abs[5] * q_a + g_abs[2] * q_r
    return divergence(h_z, h_a, h_r, absolute) + g_abs[6]


def pair_sum(padded, axis):
    length = padded.shape[axis] - 2
    core = lax.slice_in_dim(padded, 1, length + 1, axis=axis)
    upper = lax.slice_in_dim(padded, 2, length + 2, axis=axis)
    lower = lax.slice_in_dim(padded, 0, length, axis=axis)
    node = lax.broadcasted_iota(jnp.int32, core.shape, axis) % 8
    return core + jnp.where(node == 7, upper, 0.0) + jnp.where(node == 0, lower, 0.0)


def point_weight(pipe_len, cycle_len, radial_len):
    one = jnp.float32(1.0)
    two = jnp.float32(2.0)
    pipe_node = jnp.arange(pipe_len) % 8
    cycle_node = jnp.arange(cycle_len) % 8
    radial_index = jnp.arange(radial_len)
    radial_node = radial_index % 8
    count_z = jnp.where((pipe_node == 0) | (pipe_node == 7), two, one)
    count_a = jnp.where((cycle_node == 0) | (cycle_node == 7), two, one)
    inside = (radial_index > 0) & (radial_index < radial_len - 1)
    count_r = jnp.where(((radial_node == 0) | (radial_node == 7)) & inside, two, one)
    return one / (count_z[:, None, None] * count_a[None, :, None] * count_r[None, None, :])


def reference(load, geom, element_order):
    derivative = jnp.asarray(gll_derivative(), dtype=jnp.float32)
    device_base = (jnp.arange(N_WIDE * N_NARROW, dtype=jnp.int32) * E_DEV).reshape(N_WIDE, N_NARROW, 1)
    inverse = jnp.argsort(element_order, axis=-1).astype(jnp.int32)
    flat_inverse = (inverse + device_base).reshape(-1)
    flat_order = (element_order.astype(jnp.int32) + device_base).reshape(-1)
    pipe_len = EZ * 8
    cycle_len = N_NARROW * EA * 8
    radial_len = ER * 8

    placed = jnp.take(load, flat_inverse, axis=0)
    load_grid = placed.reshape(N_WIDE, N_NARROW, EZ, EA, ER, 8, 8, 8).transpose(0, 2, 5, 1, 3, 6, 4, 7)
    load_grid = load_grid.reshape(N_WIDE, pipe_len, cycle_len, radial_len)
    placed_geom = jnp.take(geom, flat_inverse, axis=1)
    metric = placed_geom.reshape(7, N_WIDE, N_NARROW, EZ, EA, ER, 8, 8, 8).transpose(1, 0, 3, 6, 2, 4, 7, 5, 8)
    metric = metric.reshape(N_WIDE, 7, pipe_len, cycle_len, radial_len)

    def assemble(blocks):
        whole = blocks.reshape(N_WIDE * pipe_len, cycle_len, radial_len)
        padded = jnp.pad(whole, ((1, 1), (1, 1), (0, 0)), mode="wrap")
        merged = pair_sum(pair_sum(padded, 0), 1)
        radial = jnp.pad(merged, ((0, 0), (0, 0), (1, 1)))
        return pair_sum(radial, 2).reshape(blocks.shape)

    def operator(blocks):
        local = lax.map(lambda pair: element_apply(pair[0], pair[1], derivative), (blocks, metric))
        return assemble(local)

    bound = assemble(lax.map(lambda block: element_bound(block, derivative), metric))
    bound_inverse = 1.0 / bound
    weight = point_weight(pipe_len, cycle_len, radial_len)[None]

    def inner(first_field, second_field):
        return jnp.sum(first_field * second_field * weight)

    center = (interval_high + interval_low) / 2.0
    half_width = (interval_high - interval_low) / 2.0
    sigma_ratio = center / half_width

    def precondition(res):
        rho_now = 1.0 / sigma_ratio
        update = res * bound_inverse / center
        result = update
        for degree_step in range(CHEB - 1):
            rho_next = 1.0 / (2.0 * sigma_ratio - rho_now)
            update = rho_next * rho_now * update + (2.0 * rho_next / half_width) * bound_inverse * (res - operator(result))
            result = result + update
            rho_now = rho_next
        return result

    grid_residual = assemble(load_grid)
    grid_solution = jnp.zeros_like(grid_residual)
    direction = grid_residual
    previous = jnp.float32(1.0)
    for iteration in range(ITERS):
        smoothed = precondition(grid_residual)
        precond_norm = inner(grid_residual, smoothed)
        if iteration == 0:
            direction = smoothed
        else:
            direction = smoothed + (precond_norm / previous) * direction
        image = operator(direction)
        step_size = precond_norm / inner(direction, image)
        grid_solution = grid_solution + step_size * direction
        grid_residual = grid_residual - step_size * image
        previous = precond_norm

    def read_back(blocks):
        rows = blocks.reshape(N_WIDE, EZ, 8, N_NARROW, EA, 8, ER, 8).transpose(0, 3, 1, 4, 6, 2, 5, 7)
        return jnp.take(rows.reshape(ELEMS, 512), flat_order, axis=0)

    return read_back(grid_solution), read_back(grid_residual)
```

```python
import functools

import jax
import jax.numpy as jnp
import numpy as np
from jax import lax
from jax.experimental import pallas as pl
from jax.experimental.pallas import tpu as pltpu
from jax.sharding import PartitionSpec as P

MESH = pl.DeviceIdType.MESH
interval_low = 0.03
interval_high = 1.0
FIELDS = 8
F32 = jnp.float32


def legendre_seven(point):
    before = 1.0
    current = point
    for degree in range(1, 7):
        after = ((2.0 * degree + 1.0) * point * current - degree * before) / (degree + 1.0)
        before = current
        current = after
    return current


def gll_derivative():
    points = 8
    inner_nodes = [
        -0.8717401485096066,
        -0.5917001814331423,
        -0.2092992179024789,
        0.2092992179024789,
        0.5917001814331423,
        0.8717401485096066,
    ]
    nodes = [-1.0] + inner_nodes + [1.0]
    values_at = [legendre_seven(node) for node in nodes]
    matrix = np.zeros((points, points))
    for source in range(points):
        for target in range(points):
            if source != target:
                matrix[source, target] = values_at[source] / (
                    values_at[target] * (nodes[source] - nodes[target])
                )
    matrix[0, 0] = -(points - 1) * points / 4.0
    matrix[points - 1, points - 1] = (points - 1) * points / 4.0
    return matrix


DERIV = gll_derivative()
ABS = np.abs(DERIV)
ROW_TOTAL = ABS.sum(axis=1)


def halves(matrix):
    even = (matrix[:4, :4] + matrix[:4, :3:-1]) / 2.0
    odd = (matrix[:4, :4] - matrix[:4, :3:-1]) / 2.0
    return even, odd


def combine(row, terms):
    total = terms[0] * float(row[0])
    for factor, term in zip(row[1:], terms[1:]):
        total = total + term * float(factor)
    return total


def along_eight(values, matrix, parity):
    even, odd = halves(matrix)
    sums = [values[m] + values[7 - m] for m in range(4)]
    differences = [values[m] - values[7 - m] for m in range(4)]
    result = [None] * 8
    for i in range(4):
        e = combine(even[i], sums)
        o = combine(odd[i], differences)
        result[i] = e + o
        result[7 - i] = (e - o) if parity > 0 else (o - e)
    return result


def lane_roll(value, shift):
    shape = value.shape
    flat = value.reshape(-1, shape[-1])
    return pltpu.roll(flat, shift, 1).reshape(shape)


def along_mirrored(value, matrix, sign):
    even, odd = halves(matrix)
    other = lane_roll(value, 64)
    plus, minus = value + other, value - other
    sums, differences = (plus, minus) if sign > 0 else (minus, plus)
    rows = []
    for j in range(4):
        rows.append(
            combine(even[j], [sums[m] for m in range(4)])
            + combine(odd[j], [differences[m] for m in range(4)])
        )
    return jnp.stack(rows)


def wide_factors(count):
    factors = []
    while count > 1:
        for factor in (4, 3, 2, 5, 7):
            if count % factor == 0:
                break
        else:
            factor = count
        factors.append(factor)
        count //= factor
    return factors


def body(
    n_wide,
    n_narrow,
    load_ref,
    geom_ref,
    order_ref,
    solution_ref,
    residual_ref,
    metric,
    work,
    radial_in,
    radial_out,
    fields,
    faces,
    res,
    binv,
    zed,
    dee,
    image,
    first,
    part,
    from_z,
    from_a,
    from_c,
    gathered,
    z_send,
    z_recv,
    a_send,
    a_recv,
    c_send,
    c_recv,
    g_send,
    g_recv,
):
    w = lax.axis_index("wide")
    n = lax.axis_index("narrow")
    up = lax.rem(w + 1, n_wide)
    down = lax.rem(w + n_wide - 1, n_wide)
    if n_narrow == 2:
        sides = [(lax.rem(n + 1, 2), 0)]
    else:
        sides = [(lax.rem(n + 1, n_narrow), 1), (lax.rem(n + n_narrow - 1, n_narrow), 2)]

    phases = []
    stride = 1
    for number, factor in enumerate(wide_factors(n_wide)):
        place = lax.rem(w // stride, factor)
        base = w - place * stride
        partners = []
        for dn in range(n_narrow if number == 0 else 1):
            for dw in range(factor):
                if dn == 0 and dw == 0:
                    continue
                there = base + lax.rem(place + dw, factor) * stride
                partners.append((there, lax.rem(n + dn, n_narrow)))
        phases.append(partners)
        stride *= factor

    barrier = pltpu.get_barrier_semaphore()
    greeted = [(up, n), (down, n)]
    for side, _ in sides:
        greeted += [(up, side), (down, side), (w, side)]
    for partners in phases:
        greeted += partners
    for device in greeted:
        pl.semaphore_signal(barrier, inc=1, device_id=device, device_id_type=MESH)

    lane = lax.broadcasted_iota(jnp.int32, (8, 128), 1)
    node = lax.broadcasted_iota(jnp.int32, (8, 128), 0)
    radial = lane % 16
    lane_row = lax.broadcasted_iota(jnp.int32, (1, 128), 1)
    mirror = jnp.where(lane_row < 64, 1.0, -1.0).astype(F32)
    radial_row = lane_row % 16

    order = order_ref[0].astype(jnp.int32)
    order_twice = jnp.concatenate([order, order + 64], axis=1)
    hot_t = (lax.broadcasted_iota(jnp.int32, (128, 128), 0) == order_twice).astype(F32)
    hot = jnp.transpose(hot_t)
    hot_both = (hot[:64] + hot[64:]).astype(jnp.bfloat16)
    top, bottom = hot[:64], hot[64:]
    zero = jnp.zeros_like(top)
    into_low = jnp.concatenate(
        [jnp.concatenate([top, zero], axis=1), jnp.concatenate([zero, top], axis=1)], axis=0
    ).astype(jnp.bfloat16)
    into_high = jnp.concatenate(
        [jnp.concatenate([bottom, zero], axis=1), jnp.concatenate([zero, bottom], axis=1)], axis=0
    ).astype(jnp.bfloat16)

    def place_pair(one, two):
        turned = jnp.transpose(jnp.concatenate([one, two], axis=0)).astype(jnp.bfloat16)
        split = turned.reshape(8, 8, 8, 128)
        low = split[:, :4].reshape(256, 128)
        high = jnp.stack([split[:, 7 - j] for j in range(4)], axis=1).reshape(256, 128)
        both = jnp.dot(low, into_low, preferred_element_type=F32)
        both = both + jnp.dot(high, into_high, preferred_element_type=F32)
        return both[:, :128], both[:, 128:]

    def rounded(value):
        return value.astype(jnp.bfloat16).astype(F32)

    load = load_ref[...]
    load_high = rounded(load)
    load_rest = load - load_high
    load_mid = rounded(load_rest)
    load_low = rounded(load_rest - load_mid)
    g = [geom_ref[q].astype(F32) for q in range(7)]
    for q in (0, 2, 4):
        metric[q], metric[q + 1] = place_pair(g[q], g[q + 1])
    metric[6], grid_high = place_pair(g[6], load_high)
    grid_mid, grid_low = place_pair(load_mid, load_low)
    fields[0] = grid_high + (grid_mid + grid_low)

    def slab(ref, i):
        return ref[pl.ds(32 * i, 32), :].reshape(4, 8, 128)

    def put(ref, i, value):
        ref[pl.ds(32 * i, 32), :] = value.reshape(32, 128)

    def radial_apply(matrix, parity):
        values = [radial_in[pl.ds(k, 32, stride=8), :] for k in range(8)]
        result = along_eight(values, matrix, parity)
        for k in range(8):
            radial_out[pl.ds(k, 32, stride=8), :] = result[k]

    q_r = jnp.full((8, 128), float(ROW_TOTAL[0]), F32)
    for k in range(1, 4):
        q_r = jnp.where((node == k) | (node == 7 - k), float(ROW_TOTAL[k]), q_r)
    h_z, part_a = [], []
    for i in range(8):
        a = [jnp.abs(slab(metric.at[q], i)) for q in range(6)]
        q_z = float(ROW_TOTAL[i])

        def by_cycle(value):
            return jnp.stack([value[j] * float(ROW_TOTAL[j]) for j in range(4)])

        h_z.append(a[0] * q_z + by_cycle(a[3]) + a[4] * q_r)
        part_a.append(along_mirrored(a[3] * q_z + by_cycle(a[1]) + a[5] * q_r, ABS.T, 1))
        put(radial_in, i, a[4] * q_z + by_cycle(a[5]) + a[2] * q_r)
    radial_apply(ABS.T, 1)
    part_z = along_eight(h_z, ABS.T, 1)
    for i in range(8):
        put(fields.at[1], i, part_z[i] + part_a[i] + slab(radial_out, i) + jnp.abs(slab(metric.at[6], i)))
    for q in (3, 5):
        metric[q] = metric[q] * mirror

    def element_apply(source, f):
        v = [slab(source, i) for i in range(8)]
        values = [source[pl.ds(k, 32, stride=8), :] for k in range(8)]
        result = along_eight(values, DERIV, -1)
        for k in range(8):
            radial_out[pl.ds(k, 32, stride=8), :] = result[k]
        grad_z = along_eight(v, DERIV, -1)
        flux_z, part_a = [], []
        for i in range(8):
            grad_a = along_mirrored(v[i], DERIV, 1)
            grad_r = slab(radial_out, i)
            g = [slab(metric.at[q], i) for q in range(6)]
            flux_z.append(g[0] * grad_z[i] + g[3] * grad_a + g[4] * grad_r)
            flux_a = g[3] * grad_z[i] + g[1] * grad_a + g[5] * grad_r
            put(radial_in, i, g[4] * grad_z[i] + g[5] * grad_a + g[2] * grad_r)
            part_a.append(along_mirrored(flux_a, DERIV.T, -1) + slab(metric.at[6], i) * v[i])
        radial_apply(DERIV.T, -1)
        part_z = along_eight(flux_z, DERIV.T, -1)
        energy = None
        for i in range(8):
            total = part_z[i] + part_a[i] + slab(radial_out, i)
            put(fields.at[f], i, total)
            term = jnp.sum(total * v[i], axis=0)
            energy = term if energy is None else energy + term
        return energy

    def assemble_own(f):
        ref = fields.at[f]
        inner = ref[pl.ds(0, 32, stride=8), :]
        outer = ref[pl.ds(7, 32, stride=8), :]
        ref[pl.ds(0, 32, stride=8), :] = inner + jnp.where(radial_row > 0, pltpu.roll(outer, 1, 1), 0.0)
        ref[pl.ds(7, 32, stride=8), :] = outer + jnp.where(radial_row < 15, pltpu.roll(inner, 127, 1), 0.0)
        for i in range(8):
            row = ref[pl.ds(32 * i, 8), :]
            below = pltpu.roll(row, 16, 1)
            above = pltpu.roll(row, 112, 1)
            for s, (_, kind) in enumerate(sides):
                message = jnp.zeros_like(row)
                if kind in (0, 1):
                    message = jnp.where(lane < 16, below, message)
                if kind in (0, 2):
                    message = jnp.where(lane >= 112, above, message)
                faces[f, s, pl.ds(8 * i, 8), :] = message
            inside = jnp.where(
                lane < 64, pltpu.roll(row, 80, 1), pltpu.roll(row, 48, 1)
            )
            ref[pl.ds(32 * i, 8), :] = row + jnp.where((lane >= 16) & (lane < 112), inside, 0.0)

    started = []

    def send(src, dst, send_sem, recv_sem, device):
        copy = pltpu.make_async_remote_copy(
            src_ref=src, dst_ref=dst, send_sem=send_sem, recv_sem=recv_sem, device_id=device, device_id_type=MESH
        )
        copy.start()
        started.append(copy)
        return copy

    def send_faces(f):
        copies = [
            send(fields.at[f, pl.ds(0, 32)], from_z.at[f, 1], z_send.at[f, 1], z_recv.at[f, 1], (down, n)),
            send(fields.at[f, pl.ds(224, 32)], from_z.at[f, 0], z_send.at[f, 0], z_recv.at[f, 0], (up, n)),
        ]
        for s, (side, _) in enumerate(sides):
            copies += [
                send(faces.at[f, s, pl.ds(0, 8)], from_c.at[f, s, 1], c_send.at[f, s, 1], c_recv.at[f, s, 1], (down, side)),
                send(faces.at[f, s, pl.ds(56, 8)], from_c.at[f, s, 0], c_send.at[f, s, 0], c_recv.at[f, s, 0], (up, side)),
            ]
        for s, (side, _) in enumerate(sides):
            copies.append(send(faces.at[f, s], from_a.at[f, s], a_send.at[f, s], a_recv.at[f, s], (w, side)))
        return copies

    def assembled(f, copies):
        for copy in copies:
            copy.wait_recv()
        result = []
        for i in range(8):
            value = slab(fields.at[f], i)
            if i == 0:
                value = value + from_z[f, 0].reshape(4, 8, 128)
            if i == 7:
                value = value + from_z[f, 1].reshape(4, 8, 128)
            row = value[0]
            for s in range(len(sides)):
                row = row + from_a[f, s, pl.ds(8 * i, 8), :]
                if i == 0:
                    row = row + from_c[f, s, 0]
                if i == 7:
                    row = row + from_c[f, s, 1]
            result.append(jnp.concatenate([row[None], value[1:]], axis=0))
        return result

    def weighted(one, two):
        total = None
        for i in range(8):
            product = one(i) * two(i)
            term = (product[1] + product[2]) + product[3] + product[0] * 0.5
            if i in (0, 7):
                term = term * 0.5
            total = term if total is None else total + term
        shared = ((node == 0) & (radial > 0)) | ((node == 7) & (radial < 15))
        return jnp.where(shared, total * 0.5, total)

    def stack_rows(terms):
        out = jnp.zeros((8, 128), F32)
        for q, term in enumerate(terms):
            out = jnp.where(node == q, jnp.sum(term, axis=0, keepdims=True), out)
        return out

    counts = [len(partners) for partners in phases]

    def sum_start(r, p, value):
        part[r, p] = value
        at = sum(counts[:p])
        return [
            send(part.at[r, p], gathered.at[r, at + q], g_send.at[r, at + q], g_recv.at[r, at + q], device)
            for q, device in enumerate(phases[p])
        ]

    def sum_end(r, p, copies):
        at = sum(counts[:p])
        total = part[r, p]
        for q, copy in enumerate(copies):
            copy.wait_recv()
            total = total + gathered[r, at + q]
        return total

    def sum_rest(r, p, copies):
        total = sum_end(r, p, copies)
        for later in range(p + 1, len(phases)):
            total = sum_end(r, later, sum_start(r, later, total))
        return jnp.sum(total, axis=1, keepdims=True)

    center = (interval_high + interval_low) / 2.0
    half_width = (interval_high - interval_low) / 2.0
    sigma = center / half_width
    rhos = [1.0 / sigma]
    for _ in range(2):
        rhos.append(1.0 / (2.0 * sigma - rhos[-1]))

    assemble_own(0)
    assemble_own(1)
    pl.semaphore_wait(barrier, len(greeted))
    copies = [send_faces(0), send_faces(1)]
    load_whole = assembled(0, copies[0])
    bound_whole = assembled(1, copies[1])
    for i in range(8):
        inverse = 1.0 / bound_whole[i]
        update = load_whole[i] * inverse * (1.0 / center)
        put(binv, i, inverse)
        put(res, i, load_whole[i])
        put(zed, i, update)
        put(dee, i, update)

    def smooth(f, source, step, between=None):
        element_apply(zed, f)
        assemble_own(f)
        copies = send_faces(f)
        after = between() if between is not None else None
        whole = assembled(f, copies)
        now, later = rhos[step], rhos[step + 1]
        for i in range(8):
            update = slab(dee, i) * (now * later) + slab(binv, i) * (slab(source, i) - whole[i]) * (
                2.0 * later / half_width
            )
            put(dee, i, update)
            put(zed, i, slab(zed, i) + update)
        return after

    smooth(2, res, 0)
    smooth(3, res, 1)
    first[...] = zed[...]
    norm = weighted(lambda i: slab(res, i), lambda i: slab(zed, i))
    energy = element_apply(zed, 4)
    assemble_own(4)
    copies = send_faces(4)
    sums = sum_start(0, 0, stack_rows([norm, energy]))
    whole = assembled(4, copies)
    for i in range(8):
        put(image, i, whole[i])
        update = whole[i] * slab(binv, i) * (1.0 / center)
        put(zed, i, update)
        put(dee, i, update)

    def next_phase():
        total = sum_end(0, 0, sums)
        return sum_start(0, 1, total)

    more = smooth(5, image, 0, next_phase)
    smooth(6, image, 1)
    total = sum_rest(0, 1, more)
    norm_0, energy_0 = total[0:1], total[1:2]
    alpha_0 = norm_0 / energy_0
    for i in range(8):
        put(res, i, slab(res, i) - alpha_0 * slab(image, i))
        put(zed, i, slab(first, i) - alpha_0 * slab(zed, i))
    norm = weighted(lambda i: slab(res, i), lambda i: slab(zed, i))
    cross = weighted(lambda i: slab(zed, i), lambda i: slab(image, i))
    energy = element_apply(zed, 7)
    assemble_own(7)
    copies = send_faces(7)
    sums = sum_start(1, 0, stack_rows([norm, cross, energy]))
    total = sum_rest(1, 0, sums)
    whole = assembled(7, copies)
    norm_1, cross_1, energy_1 = total[0:1], total[1:2], total[2:3]
    beta = norm_1 / norm_0
    alpha_1 = norm_1 / (energy_1 + 2.0 * beta * cross_1 + beta * beta * energy_0)

    def give(ref, value_of):
        rows = []
        for i in range(8):
            value = value_of(i)
            for j in range(8):
                keep = (lane < 64) if j < 4 else (lane >= 64)
                rows.append(jnp.where(keep, value[j if j < 4 else 7 - j], 0.0))
        full = jnp.stack(rows).reshape(512, 128)
        high = full.astype(jnp.bfloat16)
        low = (full - high.astype(F32)).astype(jnp.bfloat16)
        dims = (((1,), (1,)), ((), ()))
        ref[...] = lax.dot_general(hot_both, high, dims, preferred_element_type=F32) + lax.dot_general(
            hot_both, low, dims, preferred_element_type=F32
        )

    give(
        solution_ref,
        lambda i: alpha_0 * slab(first, i) + alpha_1 * (slab(zed, i) + beta * slab(first, i)),
    )
    give(residual_ref, lambda i: slab(res, i) - alpha_1 * (whole[i] + beta * slab(image, i)))
    for copy in started:
        copy.wait_send()


def solution(mesh):
    n_wide, n_narrow = mesh.shape["wide"], mesh.shape["narrow"]
    sides = 1 if n_narrow == 2 else 2
    factors = wide_factors(n_wide)
    partners = n_narrow * factors[0] - 1 + sum(factor - 1 for factor in factors[1:])
    vmem = pltpu.VMEM
    block = vmem((256, 128), F32)
    dma = pltpu.SemaphoreType.DMA

    def local(load, geom, element_order):
        whole = pl.BlockSpec(memory_space=pltpu.VMEM)
        shape = jax.ShapeDtypeStruct(load.shape, F32)
        return pl.pallas_call(
            functools.partial(body, n_wide, n_narrow),
            out_shape=(shape, shape),
            in_specs=[whole] * 3,
            out_specs=(whole, whole),
            scratch_shapes=[
                vmem((7, 256, 128), F32),
                block,
                block,
                block,
                vmem((FIELDS, 256, 128), F32),
                vmem((FIELDS, sides, 64, 128), F32),
                block,
                block,
                block,
                block,
                block,
                block,
                vmem((2, len(factors), 8, 128), F32),
                vmem((FIELDS, 2, 32, 128), F32),
                vmem((FIELDS, sides, 64, 128), F32),
                vmem((FIELDS, sides, 2, 8, 128), F32),
                vmem((2, partners, 8, 128), F32),
                dma((FIELDS, 2)),
                dma((FIELDS, 2)),
                dma((FIELDS, sides)),
                dma((FIELDS, sides)),
                dma((FIELDS, sides, 2)),
                dma((FIELDS, sides, 2)),
                dma((2, partners)),
                dma((2, partners)),
            ],
            compiler_params=pltpu.CompilerParams(
                collective_id=0, has_side_effects=True, vmem_limit_bytes=32 * 1024 * 1024
            ),
        )(load, geom, element_order)

    return jax.shard_map(
        local,
        mesh=mesh,
        in_specs=(
            P(("wide", "narrow"), None),
            P(None, ("wide", "narrow"), None),
            P("wide", "narrow", None),
        ),
        out_specs=(P(("wide", "narrow"), None), P(("wide", "narrow"), None)),
        check_vma=False,
    )
```

```python
import functools

import jax
import jax.numpy as jnp
import numpy as np
from jax import lax
from jax.experimental import pallas as pl
from jax.experimental.pallas import tpu as pltpu
from jax.sharding import PartitionSpec as P

MESH = pl.DeviceIdType.MESH
interval_low = 0.03
interval_high = 1.0
FIELDS = 8
F32 = jnp.float32


ORDER = [0, 7, 1, 6, 2, 5, 3, 4]
POS = [ORDER.index(i) for i in range(8)]
FACE = [0, 7]
INNER = [1, 6, 2, 5, 3, 4]


def legendre_seven(point):
    before = 1.0
    current = point
    for degree in range(1, 7):
        after = ((2.0 * degree + 1.0) * point * current - degree * before) / (degree + 1.0)
        before = current
        current = after
    return current


def gll_derivative():
    points = 8
    inner_nodes = [
        -0.8717401485096066,
        -0.5917001814331423,
        -0.2092992179024789,
        0.2092992179024789,
        0.5917001814331423,
        0.8717401485096066,
    ]
    nodes = [-1.0] + inner_nodes + [1.0]
    values_at = [legendre_seven(node) for node in nodes]
    matrix = np.zeros((points, points))
    for source in range(points):
        for target in range(points):
            if source != target:
                matrix[source, target] = values_at[source] / (
                    values_at[target] * (nodes[source] - nodes[target])
                )
    matrix[0, 0] = -(points - 1) * points / 4.0
    matrix[points - 1, points - 1] = (points - 1) * points / 4.0
    return matrix


DERIV = gll_derivative()
ABS = np.abs(DERIV)
ROW_TOTAL = ABS.sum(axis=1)


def halves(matrix):
    even = (matrix[:4, :4] + matrix[:4, :3:-1]) / 2.0
    odd = (matrix[:4, :4] - matrix[:4, :3:-1]) / 2.0
    return even, odd


def combine(row, terms):
    total = terms[0] * float(row[0])
    for factor, term in zip(row[1:], terms[1:]):
        total = total + term * float(factor)
    return total


def along_eight(values, matrix, parity):
    even, odd = halves(matrix)
    sums = [values[m] + values[7 - m] for m in range(4)]
    differences = [values[m] - values[7 - m] for m in range(4)]
    result = [None] * 8
    for i in range(4):
        e = combine(even[i], sums)
        o = combine(odd[i], differences)
        result[i] = e + o
        result[7 - i] = (e - o) if parity > 0 else (o - e)
    return result


def lane_roll(value, shift):
    shape = value.shape
    flat = value.reshape(-1, shape[-1])
    return pltpu.roll(flat, shift, 1).reshape(shape)


def along_mirrored(value, matrix, sign):
    even, odd = halves(matrix)
    other = lane_roll(value, 64)
    plus, minus = value + other, value - other
    sums, differences = (plus, minus) if sign > 0 else (minus, plus)
    rows = []
    for j in range(4):
        rows.append(
            combine(even[j], [sums[m] for m in range(4)])
            + combine(odd[j], [differences[m] for m in range(4)])
        )
    return jnp.stack(rows)


def wide_factors(count):
    factors = []
    while count > 1:
        for factor in (4, 3, 2, 5, 7):
            if count % factor == 0:
                break
        else:
            factor = count
        factors.append(factor)
        count //= factor
    return factors


def body(
    n_wide,
    n_narrow,
    load_hbm,
    geom_hbm,
    order_hbm,
    solution_ref,
    residual_ref,
    load_ref,
    geom_ref,
    order_ref,
    metric,
    radial_in,
    radial_out,
    part_fz,
    part_fa,
    part_fr,
    grad_z,
    fields,
    faces,
    res,
    binv,
    zed,
    dee,
    image,
    first,
    read,
    part,
    from_z,
    from_a,
    from_c,
    gathered,
    z_send,
    z_recv,
    a_send,
    a_recv,
    c_send,
    c_recv,
    g_send,
    g_recv,
    in_sem,
):
    fetches = [
        pltpu.make_async_copy(order_hbm, order_ref, in_sem.at[0]),
        pltpu.make_async_copy(load_hbm, load_ref, in_sem.at[1]),
        pltpu.make_async_copy(geom_hbm, geom_ref, in_sem.at[2]),
    ]
    for fetch in fetches:
        fetch.start()
    w = lax.axis_index("wide")
    n = lax.axis_index("narrow")
    up = lax.rem(w + 1, n_wide)
    down = lax.rem(w + n_wide - 1, n_wide)
    if n_narrow == 2:
        sides = [(lax.rem(n + 1, 2), 0)]
    else:
        sides = [(lax.rem(n + 1, n_narrow), 1), (lax.rem(n + n_narrow - 1, n_narrow), 2)]

    phases = []
    stride = 1
    for number, factor in enumerate(wide_factors(n_wide)):
        place = lax.rem(w // stride, factor)
        base = w - place * stride
        partners = []
        for dn in range(n_narrow if number == 0 else 1):
            for dw in range(factor):
                if dn == 0 and dw == 0:
                    continue
                there = base + lax.rem(place + dw, factor) * stride
                partners.append((there, lax.rem(n + dn, n_narrow)))
        phases.append(partners)
        stride *= factor

    barrier = pltpu.get_barrier_semaphore()
    greeted = [(up, n), (down, n)]
    for side, _ in sides:
        greeted += [(up, side), (down, side), (w, side)]
    for partners in phases:
        greeted += partners
    for device in greeted:
        pl.semaphore_signal(barrier, inc=1, device_id=device, device_id_type=MESH)

    lane = lax.broadcasted_iota(jnp.int32, (8, 128), 1)
    node = lax.broadcasted_iota(jnp.int32, (8, 128), 0)
    radial = lane % 16
    lane_row = lax.broadcasted_iota(jnp.int32, (1, 128), 1)
    mirror = jnp.where(lane_row < 64, 1.0, -1.0).astype(F32)
    radial_row = lane_row % 16

    for fetch in fetches:
        fetch.wait()
    order = order_ref[0].astype(jnp.int32)
    order_twice = jnp.concatenate([order, order + 64], axis=1)
    hot_t = (lax.broadcasted_iota(jnp.int32, (128, 128), 0) == order_twice).astype(F32)
    hot = jnp.transpose(hot_t)
    hot_both = (hot[:64] + hot[64:]).astype(jnp.bfloat16)
    top, bottom = hot[:64], hot[64:]
    zero = jnp.zeros_like(top)
    into_low = jnp.concatenate(
        [jnp.concatenate([top, zero], axis=1), jnp.concatenate([zero, top], axis=1)], axis=0
    ).astype(jnp.bfloat16)
    into_high = jnp.concatenate(
        [jnp.concatenate([bottom, zero], axis=1), jnp.concatenate([zero, bottom], axis=1)], axis=0
    ).astype(jnp.bfloat16)

    def place_pair(one, two):
        turned = jnp.transpose(jnp.concatenate([one, two], axis=0)).astype(jnp.bfloat16)
        split = turned.reshape(8, 8, 8, 128)
        low = jnp.stack([split[i, j] for i in ORDER for j in range(4)]).reshape(256, 128)
        high = jnp.stack([split[i, 7 - j] for i in ORDER for j in range(4)]).reshape(256, 128)
        both = jnp.dot(low, into_low, preferred_element_type=F32)
        both = both + jnp.dot(high, into_high, preferred_element_type=F32)
        return both[:, :128], both[:, 128:]

    def rounded(value):
        return value.astype(jnp.bfloat16).astype(F32)

    load = load_ref[...]
    load_high = rounded(load)
    load_rest = load - load_high
    load_mid = rounded(load_rest)
    load_low = rounded(load_rest - load_mid)
    g = [geom_ref[q].astype(F32) for q in range(7)]
    for q in (0, 2, 4):
        metric[q], metric[q + 1] = place_pair(g[q], g[q + 1])
    metric[6], grid_high = place_pair(g[6], load_high)
    grid_mid, grid_low = place_pair(load_mid, load_low)
    fields[0] = grid_high + (grid_mid + grid_low)

    def slab(ref, i):
        return ref[pl.ds(32 * POS[i], 32), :].reshape(4, 8, 128)

    def put(ref, i, value):
        ref[pl.ds(32 * POS[i], 32), :] = value.reshape(32, 128)

    def radial_apply(source, matrix, parity, start=0, count=32):
        values = [source[pl.ds(8 * start + k, count, stride=8), :] for k in range(8)]
        result = along_eight(values, matrix, parity)
        for k in range(8):
            radial_out[pl.ds(8 * start + k, count, stride=8), :] = result[k]

    q_r = jnp.full((8, 128), float(ROW_TOTAL[0]), F32)
    for k in range(1, 4):
        q_r = jnp.where((node == k) | (node == 7 - k), float(ROW_TOTAL[k]), q_r)
    h_z, part_a = [], []
    for i in range(8):
        a = [jnp.abs(slab(metric.at[q], i)) for q in range(6)]
        q_z = float(ROW_TOTAL[i])

        def by_cycle(value):
            return jnp.stack([value[j] * float(ROW_TOTAL[j]) for j in range(4)])

        h_z.append(a[0] * q_z + by_cycle(a[3]) + a[4] * q_r)
        part_a.append(along_mirrored(a[3] * q_z + by_cycle(a[1]) + a[5] * q_r, ABS.T, 1))
        put(radial_in, i, a[4] * q_z + by_cycle(a[5]) + a[2] * q_r)
    radial_apply(radial_in, ABS.T, 1)
    part_z = along_eight(h_z, ABS.T, 1)
    for i in range(8):
        put(fields.at[1], i, part_z[i] + part_a[i] + slab(radial_out, i) + jnp.abs(slab(metric.at[6], i)))
    for q in (3, 5):
        metric[q] = metric[q] * mirror

    even, odd = halves(DERIV)
    even_t, odd_t = halves(DERIV.T)

    def forward_inner():
        radial_apply(zed, DERIV, -1, 8, 24)
        for i in INNER:
            grad_a = along_mirrored(slab(zed, i), DERIV, 1)
            grad_r = slab(radial_out, i)
            put(part_fz, i, slab(metric.at[3], i) * grad_a + slab(metric.at[4], i) * grad_r)
            put(part_fa, i, slab(metric.at[1], i) * grad_a + slab(metric.at[5], i) * grad_r)
            put(part_fr, i, slab(metric.at[5], i) * grad_a + slab(metric.at[2], i) * grad_r)
        for j in range(4):
            v = [tile(zed, i, j) for i in range(1, 7)]
            sums = [v[m] + v[5 - m] for m in range(3)]
            differences = [v[m] - v[5 - m] for m in range(3)]
            for i in range(4):
                e, o = combine(even[i][1:], sums), combine(odd[i][1:], differences)
                put_tile(grad_z, i, j, e + o)
                put_tile(grad_z, 7 - i, j, o - e)

    def tile(ref, i, j):
        return ref[pl.ds(32 * POS[i] + 8 * j, 8), :]

    def put_tile(ref, i, j, value):
        ref[pl.ds(32 * POS[i] + 8 * j, 8), :] = value

    def forward_face(f):
        radial_apply(zed, DERIV, -1, 0, 8)
        grad_a = {i: along_mirrored(slab(zed, i), DERIV, 1) for i in FACE}
        energy = jnp.zeros((8, 128), F32)
        flux_a = {i: [] for i in FACE}
        pieces = {i: [] for i in FACE}
        for j in range(4):
            v0, v7 = tile(zed, 0, j), tile(zed, 7, j)
            plus, minus = v0 + v7, v0 - v7
            flux_z = [None] * 8
            for i in range(4):
                e, o = plus * float(even[i][0]), minus * float(odd[i][0])
                for node_i, extra in ((i, e + o), (7 - i, o - e)):
                    slope = tile(grad_z, node_i, j) + extra
                    put_tile(grad_z, node_i, j, slope)
                    if node_i in FACE:
                        g = [tile(metric.at[q], node_i, j) for q in range(6)]
                        slope_a = grad_a[node_i][j]
                        slope_r = tile(radial_out, node_i, j)
                        flux = g[0] * slope + g[3] * slope_a + g[4] * slope_r
                        flux_a[node_i].append(g[3] * slope + g[1] * slope_a + g[5] * slope_r)
                        put_tile(radial_in, node_i, j, g[4] * slope + g[5] * slope_a + g[2] * slope_r)
                    else:
                        flux = tile(part_fz, node_i, j) + tile(metric.at[0], node_i, j) * slope
                    put_tile(part_fz, node_i, j, flux)
                    flux_z[node_i] = flux
            e = combine(even_t[0], [flux_z[m] + flux_z[7 - m] for m in range(4)])
            o = combine(odd_t[0], [flux_z[m] - flux_z[7 - m] for m in range(4)])
            pieces[0].append(e + o + tile(metric.at[6], 0, j) * v0)
            pieces[7].append(o - e + tile(metric.at[6], 7, j) * v7)
        radial_apply(radial_in, DERIV.T, -1, 0, 8)
        for i in FACE:
            total = jnp.stack(pieces[i]) + along_mirrored(jnp.stack(flux_a[i]), DERIV.T, -1) + slab(radial_out, i)
            put(fields.at[f], i, total)
            energy = energy + jnp.sum(total * slab(zed, i), axis=0)
        return energy

    def forward_rest(f):
        energy = jnp.zeros((8, 128), F32)
        for i in INNER:
            slope = slab(grad_z, i)
            flux_a = slab(part_fa, i) + slab(metric.at[3], i) * slope
            put(radial_in, i, slab(part_fr, i) + slab(metric.at[4], i) * slope)
            put(part_fa, i, along_mirrored(flux_a, DERIV.T, -1) + slab(metric.at[6], i) * slab(zed, i))
        radial_apply(radial_in, DERIV.T, -1, 8, 24)
        for j in range(4):
            flux_z = [tile(part_fz, i, j) for i in range(8)]
            sums = [flux_z[m] + flux_z[7 - m] for m in range(4)]
            differences = [flux_z[m] - flux_z[7 - m] for m in range(4)]
            for i in range(1, 4):
                e, o = combine(even_t[i], sums), combine(odd_t[i], differences)
                for node_i, piece in ((i, e + o), (7 - i, o - e)):
                    total = piece + tile(part_fa, node_i, j) + tile(radial_out, node_i, j)
                    put_tile(fields.at[f], node_i, j, total)
                    energy = energy + total * tile(zed, node_i, j)
        return energy

    def assemble_own(f, start, count):
        ref = fields.at[f]
        low = pl.ds(8 * start, count, stride=8)
        high = pl.ds(8 * start + 7, count, stride=8)
        inner, outer = ref[low, :], ref[high, :]
        ref[low, :] = inner + jnp.where(radial_row > 0, pltpu.roll(outer, 1, 1), 0.0)
        ref[high, :] = outer + jnp.where(radial_row < 15, pltpu.roll(inner, 127, 1), 0.0)
        for at in range(start // 4, (start + count) // 4):
            row = ref[pl.ds(32 * at, 8), :]
            below = pltpu.roll(row, 16, 1)
            above = pltpu.roll(row, 112, 1)
            for s, (_, kind) in enumerate(sides):
                message = jnp.zeros_like(row)
                if kind in (0, 1):
                    message = jnp.where(lane < 16, below, message)
                if kind in (0, 2):
                    message = jnp.where(lane >= 112, above, message)
                faces[f, s, pl.ds(8 * at, 8), :] = message
            inside = jnp.where(lane < 64, pltpu.roll(row, 80, 1), pltpu.roll(row, 48, 1))
            ref[pl.ds(32 * at, 8), :] = row + jnp.where((lane >= 16) & (lane < 112), inside, 0.0)

    started = []

    def send(src, dst, send_sem, recv_sem, device):
        copy = pltpu.make_async_remote_copy(
            src_ref=src, dst_ref=dst, send_sem=send_sem, recv_sem=recv_sem, device_id=device, device_id_type=MESH
        )
        copy.start()
        started.append(copy)
        return copy

    def send_pipe(f):
        copies = [
            send(fields.at[f, pl.ds(0, 32)], from_z.at[f, 1], z_send.at[f, 1], z_recv.at[f, 1], (down, n)),
            send(fields.at[f, pl.ds(32, 32)], from_z.at[f, 0], z_send.at[f, 0], z_recv.at[f, 0], (up, n)),
        ]
        for s, (side, _) in enumerate(sides):
            copies += [
                send(faces.at[f, s, pl.ds(0, 8)], from_c.at[f, s, 1], c_send.at[f, s, 1], c_recv.at[f, s, 1], (down, side)),
                send(faces.at[f, s, pl.ds(8, 8)], from_c.at[f, s, 0], c_send.at[f, s, 0], c_recv.at[f, s, 0], (up, side)),
            ]
        return copies

    def send_cycle(f):
        return [
            send(faces.at[f, s], from_a.at[f, s], a_send.at[f, s], a_recv.at[f, s], (w, side))
            for s, (side, _) in enumerate(sides)
        ]

    def whole_plane(f, i):
        value = slab(fields.at[f], i)
        row = value[0]
        for s in range(len(sides)):
            row = row + from_a[f, s, pl.ds(8 * POS[i], 8), :]
        if i in FACE:
            come = from_z[f, POS[i]].reshape(4, 8, 128)
            row = row + come[0]
            for s in range(len(sides)):
                row = row + from_c[f, s, POS[i]]
            return jnp.concatenate([row[None], value[1:] + come[1:]], axis=0)
        return jnp.concatenate([row[None], value[1:]], axis=0)

    def wait_all(copies):
        for copy in copies:
            copy.wait_recv()

    def weighted(one, two):
        total = None
        for i in range(8):
            product = one(i) * two(i)
            term = (product[1] + product[2]) + product[3] + product[0] * 0.5
            if i in (0, 7):
                term = term * 0.5
            total = term if total is None else total + term
        shared = ((node == 0) & (radial > 0)) | ((node == 7) & (radial < 15))
        return jnp.where(shared, total * 0.5, total)

    def stack_rows(terms):
        out = jnp.zeros((8, 128), F32)
        for q, term in enumerate(terms):
            out = jnp.where(node == q, jnp.sum(term, axis=0, keepdims=True), out)
        return out

    counts = [len(partners) for partners in phases]

    def sum_start(r, p, value):
        part[r, p] = value
        at = sum(counts[:p])
        return [
            send(part.at[r, p], gathered.at[r, at + q], g_send.at[r, at + q], g_recv.at[r, at + q], device)
            for q, device in enumerate(phases[p])
        ]

    def sum_end(r, p, copies):
        at = sum(counts[:p])
        total = part[r, p]
        for q, copy in enumerate(copies):
            copy.wait_recv()
            total = total + gathered[r, at + q]
        return total

    def sum_rest(r, p, copies):
        total = sum_end(r, p, copies)
        for later in range(p + 1, len(phases)):
            total = sum_end(r, later, sum_start(r, later, total))
        return jnp.sum(total, axis=1, keepdims=True)

    center = (interval_high + interval_low) / 2.0
    half_width = (interval_high - interval_low) / 2.0
    sigma = center / half_width
    rhos = [1.0 / sigma]
    for _ in range(2):
        rhos.append(1.0 / (2.0 * sigma - rhos[-1]))

    assemble_own(0, 0, 32)
    assemble_own(1, 0, 32)
    pl.semaphore_wait(barrier, len(greeted))
    pipe = send_pipe(1) + send_pipe(0)
    cycle = send_cycle(1) + send_cycle(0)

    def begin(i):
        inverse = 1.0 / whole_plane(1, i)
        load_plane = whole_plane(0, i)
        update = load_plane * inverse * (1.0 / center)
        put(binv, i, inverse)
        put(res, i, load_plane)
        put(zed, i, update)
        put(dee, i, update)

    wait_all(cycle)
    for i in INNER:
        begin(i)
    forward_inner()
    wait_all(pipe)
    for i in FACE:
        begin(i)

    def apply_then(f, update, between=None, last=None):
        energy = forward_face(f)
        assemble_own(f, 0, 8)
        pipe = send_pipe(f)
        energy = energy + forward_rest(f)
        assemble_own(f, 8, 24)
        cycle = send_cycle(f)
        after = between(energy) if between is not None else None
        wait_all(cycle)
        for i in INNER:
            update(i, whole_plane(f, i))
        forward_inner()
        wait_all(pipe)
        for i in FACE:
            update(i, whole_plane(f, i))
        return after

    def smoothed(source, step, i, plane):
        now, later = rhos[step], rhos[step + 1]
        return slab(dee, i) * (now * later) + slab(binv, i) * (slab(source, i) - plane) * (2.0 * later / half_width)

    def smooth(source, step):
        def update(i, plane):
            change = smoothed(source, step, i, plane)
            put(dee, i, change)
            put(zed, i, slab(zed, i) + change)

        return update

    apply_then(2, smooth(res, 0))
    apply_then(3, smooth(res, 1))

    def start_norm(energy):
        norm = weighted(lambda i: slab(res, i), lambda i: slab(zed, i))
        return sum_start(0, 0, stack_rows([norm, energy]))

    def restart(i, plane):
        put(image, i, plane)
        put(first, i, slab(zed, i))
        update = plane * slab(binv, i) * (1.0 / center)
        put(zed, i, update)
        put(dee, i, update)

    sums = apply_then(4, restart, start_norm)
    more = apply_then(5, smooth(image, 0), lambda energy: sum_start(0, 1, sum_end(0, 0, sums)))
    scalars = {}

    def finish_norm(energy):
        total = sum_rest(0, 1, more)
        scalars["norm"], scalars["energy"] = total[0:1], total[1:2]
        scalars["alpha"] = total[0:1] / total[1:2]

    def step_on(i, plane):
        end = slab(zed, i) + smoothed(image, 1, i, plane)
        put(res, i, slab(res, i) - scalars["alpha"] * slab(image, i))
        put(zed, i, slab(first, i) - scalars["alpha"] * end)

    apply_then(6, step_on, finish_norm)
    norm_0, energy_0, alpha_0 = scalars["norm"], scalars["energy"], scalars["alpha"]

    def read_back(value_of, planes):
        rows = []
        for i in planes:
            value = value_of(i)
            for j in range(8):
                keep = (lane < 64) if j < 4 else (lane >= 64)
                rows.append(jnp.where(keep, value[j if j < 4 else 7 - j], 0.0))
        full = jnp.stack(rows).reshape(64 * len(planes), 128)
        high = full.astype(jnp.bfloat16)
        low = (full - high.astype(F32)).astype(jnp.bfloat16)
        dims = (((1,), (1,)), ((), ()))
        return lax.dot_general(hot_both, high, dims, preferred_element_type=F32) + lax.dot_general(
            hot_both, low, dims, preferred_element_type=F32
        )

    energy = forward_face(7)
    assemble_own(7, 0, 8)
    pipe = send_pipe(7)
    energy = energy + forward_rest(7)
    norm = weighted(lambda i: slab(res, i), lambda i: slab(zed, i))
    cross = weighted(lambda i: slab(zed, i), lambda i: slab(image, i))
    sums = sum_start(1, 0, stack_rows([norm, cross, energy]))
    assemble_own(7, 8, 24)
    cycle = send_cycle(7)
    for q, ref in enumerate((first, zed)):
        read[q] = read_back(lambda i: slab(ref, i), range(8))
    totals = sum_end(1, 0, sums)
    for later in range(1, len(phases) - 1):
        totals = sum_end(1, later, sum_start(1, later, totals))
    sums = sum_start(1, len(phases) - 1, totals)
    for q, ref in enumerate((res, image)):
        read[2 + q] = read_back(lambda i: slab(ref, i), range(8))
    wait_all(cycle)
    middle = read_back(lambda i: whole_plane(7, i), range(2, 6))
    total = jnp.sum(sum_end(1, len(phases) - 1, sums), axis=1, keepdims=True)
    norm_1, cross_1, energy_1 = total[0:1], total[1:2], total[2:3]
    beta = norm_1 / norm_0
    alpha_1 = norm_1 / (energy_1 + 2.0 * beta * cross_1 + beta * beta * energy_0)
    solution_ref[...] = (alpha_0 + alpha_1 * beta) * read[0] + alpha_1 * read[1]
    residual = read[2] - (alpha_1 * beta) * read[3]
    residual_ref[:, 128:384] = residual[:, 128:384] - alpha_1 * middle
    wait_all(pipe)
    ends = read_back(lambda i: whole_plane(7, i), (0, 1, 6, 7))
    residual_ref[:, 0:128] = residual[:, 0:128] - alpha_1 * ends[:, 0:128]
    residual_ref[:, 384:512] = residual[:, 384:512] - alpha_1 * ends[:, 128:256]
    for copy in started:
        copy.wait_send()


def solution(mesh):
    n_wide, n_narrow = mesh.shape["wide"], mesh.shape["narrow"]
    sides = 1 if n_narrow == 2 else 2
    factors = wide_factors(n_wide)
    partners = n_narrow * factors[0] - 1 + sum(factor - 1 for factor in factors[1:])
    vmem = pltpu.VMEM
    block = vmem((256, 128), F32)
    dma = pltpu.SemaphoreType.DMA

    def local(load, geom, element_order):
        whole = pl.BlockSpec(memory_space=pltpu.VMEM)
        shape = jax.ShapeDtypeStruct(load.shape, F32)
        return pl.pallas_call(
            functools.partial(body, n_wide, n_narrow),
            out_shape=(shape, shape),
            in_specs=[pl.BlockSpec(memory_space=pltpu.HBM)] * 3,
            out_specs=(whole, whole),
            scratch_shapes=[
                vmem(load.shape, F32),
                vmem(geom.shape, geom.dtype),
                vmem(element_order.shape, jnp.int32),
                vmem((7, 256, 128), F32),
                block,
                block,
                block,
                block,
                block,
                block,
                vmem((FIELDS, 256, 128), F32),
                vmem((FIELDS, sides, 64, 128), F32),
                block,
                block,
                block,
                block,
                block,
                block,
                vmem((4, 64, 512), F32),
                vmem((2, len(factors), 8, 128), F32),
                vmem((FIELDS, 2, 32, 128), F32),
                vmem((FIELDS, sides, 64, 128), F32),
                vmem((FIELDS, sides, 2, 8, 128), F32),
                vmem((2, partners, 8, 128), F32),
                dma((FIELDS, 2)),
                dma((FIELDS, 2)),
                dma((FIELDS, sides)),
                dma((FIELDS, sides)),
                dma((FIELDS, sides, 2)),
                dma((FIELDS, sides, 2)),
                dma((2, partners)),
                dma((2, partners)),
                dma((3,)),
            ],
            compiler_params=pltpu.CompilerParams(
                collective_id=0, has_side_effects=True, vmem_limit_bytes=32 * 1024 * 1024
            ),
        )(load, geom, element_order)

    return jax.shard_map(
        local,
        mesh=mesh,
        in_specs=(
            P(("wide", "narrow"), None),
            P(None, ("wide", "narrow"), None),
            P("wide", "narrow", None),
        ),
        out_specs=(P(("wide", "narrow"), None), P(("wide", "narrow"), None)),
        check_vma=False,
    )
```

```python
import functools

import jax
import jax.numpy as jnp
import numpy as np
from jax import lax
from jax.experimental import pallas as pl
from jax.experimental.pallas import tpu as pltpu
from jax.sharding import PartitionSpec as P

MESH = pl.DeviceIdType.MESH
interval_low = 0.03
interval_high = 1.0
FIELDS = 8
F32 = jnp.float32


ORDER = [0, 7, 1, 6, 2, 5, 3, 4]
POS = [ORDER.index(i) for i in range(8)]
FACE = [0, 7]
INNER = [1, 6, 2, 5, 3, 4]


def legendre_seven(point):
    before = 1.0
    current = point
    for degree in range(1, 7):
        after = ((2.0 * degree + 1.0) * point * current - degree * before) / (degree + 1.0)
        before = current
        current = after
    return current


def gll_derivative():
    points = 8
    inner_nodes = [
        -0.8717401485096066,
        -0.5917001814331423,
        -0.2092992179024789,
        0.2092992179024789,
        0.5917001814331423,
        0.8717401485096066,
    ]
    nodes = [-1.0] + inner_nodes + [1.0]
    values_at = [legendre_seven(node) for node in nodes]
    matrix = np.zeros((points, points))
    for source in range(points):
        for target in range(points):
            if source != target:
                matrix[source, target] = values_at[source] / (
                    values_at[target] * (nodes[source] - nodes[target])
                )
    matrix[0, 0] = -(points - 1) * points / 4.0
    matrix[points - 1, points - 1] = (points - 1) * points / 4.0
    return matrix


DERIV = gll_derivative()
ABS = np.abs(DERIV)
ROW_TOTAL = ABS.sum(axis=1)


def halves(matrix):
    even = (matrix[:4, :4] + matrix[:4, :3:-1]) / 2.0
    odd = (matrix[:4, :4] - matrix[:4, :3:-1]) / 2.0
    return even, odd


def combine(row, terms):
    total = terms[0] * float(row[0])
    for factor, term in zip(row[1:], terms[1:]):
        total = total + term * float(factor)
    return total


def along_eight(values, matrix, parity):
    even, odd = halves(matrix)
    sums = [values[m] + values[7 - m] for m in range(4)]
    differences = [values[m] - values[7 - m] for m in range(4)]
    result = [None] * 8
    for i in range(4):
        e = combine(even[i], sums)
        o = combine(odd[i], differences)
        result[i] = e + o
        result[7 - i] = (e - o) if parity > 0 else (o - e)
    return result


def lane_roll(value, shift):
    shape = value.shape
    flat = value.reshape(-1, shape[-1])
    return pltpu.roll(flat, shift, 1).reshape(shape)


def along_mirrored(value, matrix, sign):
    even, odd = halves(matrix)
    other = lane_roll(value, 64)
    plus, minus = value + other, value - other
    sums, differences = (plus, minus) if sign > 0 else (minus, plus)
    rows = []
    for j in range(4):
        rows.append(
            combine(even[j], [sums[m] for m in range(4)])
            + combine(odd[j], [differences[m] for m in range(4)])
        )
    return jnp.stack(rows)


def wide_factors(count):
    factors = []
    while count > 1:
        for factor in (4, 3, 2, 5, 7):
            if count % factor == 0:
                break
        else:
            factor = count
        factors.append(factor)
        count //= factor
    return factors


def body(
    n_wide,
    n_narrow,
    load_hbm,
    geom_hbm,
    order_hbm,
    solution_ref,
    residual_ref,
    load_ref,
    geom_ref,
    order_ref,
    metric,
    radial_in,
    radial_out,
    part_fz,
    part_fa,
    part_fr,
    grad_z,
    fields,
    faces,
    res,
    binv,
    zed,
    dee,
    image,
    first,
    read,
    part,
    from_z,
    from_a,
    from_c,
    gathered,
    z_send,
    z_recv,
    a_send,
    a_recv,
    c_send,
    c_recv,
    g_send,
    g_recv,
    in_sem,
):
    fetches = [
        pltpu.make_async_copy(order_hbm, order_ref, in_sem.at[0]),
        pltpu.make_async_copy(load_hbm, load_ref, in_sem.at[1]),
        pltpu.make_async_copy(geom_hbm, geom_ref, in_sem.at[2]),
    ]
    for fetch in fetches:
        fetch.start()
    w = lax.axis_index("wide")
    n = lax.axis_index("narrow")
    up = lax.rem(w + 1, n_wide)
    down = lax.rem(w + n_wide - 1, n_wide)
    if n_narrow == 2:
        sides = [(lax.rem(n + 1, 2), 0)]
    else:
        sides = [(lax.rem(n + 1, n_narrow), 1), (lax.rem(n + n_narrow - 1, n_narrow), 2)]

    phases = []
    stride = 1
    for number, factor in enumerate(wide_factors(n_wide)):
        place = lax.rem(w // stride, factor)
        base = w - place * stride
        partners = []
        for dn in range(n_narrow if number == 0 else 1):
            for dw in range(factor):
                if dn == 0 and dw == 0:
                    continue
                there = base + lax.rem(place + dw, factor) * stride
                partners.append((there, lax.rem(n + dn, n_narrow)))
        phases.append(partners)
        stride *= factor

    barrier = pltpu.get_barrier_semaphore()
    greeted = [(up, n), (down, n)]
    for side, _ in sides:
        greeted += [(up, side), (down, side), (w, side)]
    for partners in phases:
        greeted += partners
    for device in greeted:
        pl.semaphore_signal(barrier, inc=1, device_id=device, device_id_type=MESH)

    lane = lax.broadcasted_iota(jnp.int32, (8, 128), 1)
    node = lax.broadcasted_iota(jnp.int32, (8, 128), 0)
    radial = lane % 16
    lane_row = lax.broadcasted_iota(jnp.int32, (1, 128), 1)
    mirror = jnp.where(lane_row < 64, 1.0, -1.0).astype(F32)
    radial_row = lane_row % 16

    for fetch in fetches:
        fetch.wait()
    order = order_ref[0].astype(jnp.int32)
    order_twice = jnp.concatenate([order, order + 64], axis=1)
    hot_t = (lax.broadcasted_iota(jnp.int32, (128, 128), 0) == order_twice).astype(F32)
    hot = jnp.transpose(hot_t)
    hot_both = (hot[:64] + hot[64:]).astype(jnp.bfloat16)
    top, bottom = hot[:64], hot[64:]
    zero = jnp.zeros_like(top)
    into_low = jnp.concatenate(
        [jnp.concatenate([top, zero], axis=1), jnp.concatenate([zero, top], axis=1)], axis=0
    ).astype(jnp.bfloat16)
    into_high = jnp.concatenate(
        [jnp.concatenate([bottom, zero], axis=1), jnp.concatenate([zero, bottom], axis=1)], axis=0
    ).astype(jnp.bfloat16)

    def place_pair(one, two):
        turned = jnp.transpose(jnp.concatenate([one, two], axis=0)).astype(jnp.bfloat16)
        split = turned.reshape(8, 8, 8, 128)
        low = jnp.stack([split[i, j] for i in ORDER for j in range(4)]).reshape(256, 128)
        high = jnp.stack([split[i, 7 - j] for i in ORDER for j in range(4)]).reshape(256, 128)
        both = jnp.dot(low, into_low, preferred_element_type=F32)
        both = both + jnp.dot(high, into_high, preferred_element_type=F32)
        return both[:, :128], both[:, 128:]

    def rounded(value):
        return value.astype(jnp.bfloat16).astype(F32)

    load = load_ref[...]
    load_high = rounded(load)
    load_rest = load - load_high
    load_mid = rounded(load_rest)
    load_low = rounded(load_rest - load_mid)
    g = [geom_ref[q].astype(F32) for q in range(7)]
    for q in (0, 2, 4):
        metric[q], metric[q + 1] = place_pair(g[q], g[q + 1])
    metric[6], grid_high = place_pair(g[6], load_high)
    grid_mid, grid_low = place_pair(load_mid, load_low)
    fields[0] = grid_high + (grid_mid + grid_low)

    def slab(ref, i):
        return ref[pl.ds(32 * POS[i], 32), :].reshape(4, 8, 128)

    def put(ref, i, value):
        ref[pl.ds(32 * POS[i], 32), :] = value.reshape(32, 128)

    def radial_apply(source, matrix, parity, start=0, count=32):
        values = [source[pl.ds(8 * start + k, count, stride=8), :] for k in range(8)]
        result = along_eight(values, matrix, parity)
        for k in range(8):
            radial_out[pl.ds(8 * start + k, count, stride=8), :] = result[k]

    q_r = jnp.full((8, 128), float(ROW_TOTAL[0]), F32)
    for k in range(1, 4):
        q_r = jnp.where((node == k) | (node == 7 - k), float(ROW_TOTAL[k]), q_r)
    h_z, part_a = [None] * 8, [None] * 8

    def by_cycle(value):
        return jnp.stack([value[j] * float(ROW_TOTAL[j]) for j in range(4)])

    def bound_fluxes(i):
        a = [jnp.abs(slab(metric.at[q], i)) for q in range(6)]
        q_z = float(ROW_TOTAL[i])
        h_z[i] = a[0] * q_z + by_cycle(a[3]) + a[4] * q_r
        part_a[i] = along_mirrored(a[3] * q_z + by_cycle(a[1]) + a[5] * q_r, ABS.T, 1)
        put(radial_in, i, a[4] * q_z + by_cycle(a[5]) + a[2] * q_r)

    def bound_total(i, part_z):
        put(fields.at[1], i, part_z[i] + part_a[i] + slab(radial_out, i) + jnp.abs(slab(metric.at[6], i)))

    even, odd = halves(DERIV)
    even_t, odd_t = halves(DERIV.T)

    def forward_inner():
        radial_apply(zed, DERIV, -1, 8, 24)
        for i in INNER:
            grad_a = along_mirrored(slab(zed, i), DERIV, 1)
            grad_r = slab(radial_out, i)
            put(part_fz, i, slab(metric.at[3], i) * grad_a + slab(metric.at[4], i) * grad_r)
            put(part_fa, i, slab(metric.at[1], i) * grad_a + slab(metric.at[5], i) * grad_r)
            put(part_fr, i, slab(metric.at[5], i) * grad_a + slab(metric.at[2], i) * grad_r)
        for j in range(4):
            v = [tile(zed, i, j) for i in range(1, 7)]
            sums = [v[m] + v[5 - m] for m in range(3)]
            differences = [v[m] - v[5 - m] for m in range(3)]
            for i in range(4):
                e, o = combine(even[i][1:], sums), combine(odd[i][1:], differences)
                put_tile(grad_z, i, j, e + o)
                put_tile(grad_z, 7 - i, j, o - e)

    def tile(ref, i, j):
        return ref[pl.ds(32 * POS[i] + 8 * j, 8), :]

    def put_tile(ref, i, j, value):
        ref[pl.ds(32 * POS[i] + 8 * j, 8), :] = value

    def forward_face(f):
        radial_apply(zed, DERIV, -1, 0, 8)
        grad_a = {i: along_mirrored(slab(zed, i), DERIV, 1) for i in FACE}
        energy = jnp.zeros((8, 128), F32)
        flux_a = {i: [] for i in FACE}
        pieces = {i: [] for i in FACE}
        for j in range(4):
            v0, v7 = tile(zed, 0, j), tile(zed, 7, j)
            plus, minus = v0 + v7, v0 - v7
            flux_z = [None] * 8
            for i in range(4):
                e, o = plus * float(even[i][0]), minus * float(odd[i][0])
                for node_i, extra in ((i, e + o), (7 - i, o - e)):
                    slope = tile(grad_z, node_i, j) + extra
                    put_tile(grad_z, node_i, j, slope)
                    if node_i in FACE:
                        g = [tile(metric.at[q], node_i, j) for q in range(6)]
                        slope_a = grad_a[node_i][j]
                        slope_r = tile(radial_out, node_i, j)
                        flux = g[0] * slope + g[3] * slope_a + g[4] * slope_r
                        flux_a[node_i].append(g[3] * slope + g[1] * slope_a + g[5] * slope_r)
                        put_tile(radial_in, node_i, j, g[4] * slope + g[5] * slope_a + g[2] * slope_r)
                    else:
                        flux = tile(part_fz, node_i, j) + tile(metric.at[0], node_i, j) * slope
                    put_tile(part_fz, node_i, j, flux)
                    flux_z[node_i] = flux
            e = combine(even_t[0], [flux_z[m] + flux_z[7 - m] for m in range(4)])
            o = combine(odd_t[0], [flux_z[m] - flux_z[7 - m] for m in range(4)])
            pieces[0].append(e + o + tile(metric.at[6], 0, j) * v0)
            pieces[7].append(o - e + tile(metric.at[6], 7, j) * v7)
        radial_apply(radial_in, DERIV.T, -1, 0, 8)
        for i in FACE:
            total = jnp.stack(pieces[i]) + along_mirrored(jnp.stack(flux_a[i]), DERIV.T, -1) + slab(radial_out, i)
            put(fields.at[f], i, total)
            energy = energy + jnp.sum(total * slab(zed, i), axis=0)
        return energy

    def forward_rest(f):
        energy = jnp.zeros((8, 128), F32)
        for i in INNER:
            slope = slab(grad_z, i)
            flux_a = slab(part_fa, i) + slab(metric.at[3], i) * slope
            put(radial_in, i, slab(part_fr, i) + slab(metric.at[4], i) * slope)
            put(part_fa, i, along_mirrored(flux_a, DERIV.T, -1) + slab(metric.at[6], i) * slab(zed, i))
        radial_apply(radial_in, DERIV.T, -1, 8, 24)
        for j in range(4):
            flux_z = [tile(part_fz, i, j) for i in range(8)]
            sums = [flux_z[m] + flux_z[7 - m] for m in range(4)]
            differences = [flux_z[m] - flux_z[7 - m] for m in range(4)]
            for i in range(1, 4):
                e, o = combine(even_t[i], sums), combine(odd_t[i], differences)
                for node_i, piece in ((i, e + o), (7 - i, o - e)):
                    total = piece + tile(part_fa, node_i, j) + tile(radial_out, node_i, j)
                    put_tile(fields.at[f], node_i, j, total)
                    energy = energy + total * tile(zed, node_i, j)
        return energy

    def assemble_own(f, start, count):
        ref = fields.at[f]
        low = pl.ds(8 * start, count, stride=8)
        high = pl.ds(8 * start + 7, count, stride=8)
        inner, outer = ref[low, :], ref[high, :]
        ref[low, :] = inner + jnp.where(radial_row > 0, pltpu.roll(outer, 1, 1), 0.0)
        ref[high, :] = outer + jnp.where(radial_row < 15, pltpu.roll(inner, 127, 1), 0.0)
        for at in range(start // 4, (start + count) // 4):
            row = ref[pl.ds(32 * at, 8), :]
            below = pltpu.roll(row, 16, 1)
            above = pltpu.roll(row, 112, 1)
            for s, (_, kind) in enumerate(sides):
                message = jnp.zeros_like(row)
                if kind in (0, 1):
                    message = jnp.where(lane < 16, below, message)
                if kind in (0, 2):
                    message = jnp.where(lane >= 112, above, message)
                faces[f, s, pl.ds(8 * at, 8), :] = message
            inside = jnp.where(lane < 64, pltpu.roll(row, 80, 1), pltpu.roll(row, 48, 1))
            ref[pl.ds(32 * at, 8), :] = row + jnp.where((lane >= 16) & (lane < 112), inside, 0.0)

    started = []

    def send(src, dst, send_sem, recv_sem, device):
        copy = pltpu.make_async_remote_copy(
            src_ref=src, dst_ref=dst, send_sem=send_sem, recv_sem=recv_sem, device_id=device, device_id_type=MESH
        )
        copy.start()
        started.append(copy)
        return copy

    def send_pipe(f):
        copies = [
            send(fields.at[f, pl.ds(0, 32)], from_z.at[f, 1], z_send.at[f, 1], z_recv.at[f, 1], (down, n)),
            send(fields.at[f, pl.ds(32, 32)], from_z.at[f, 0], z_send.at[f, 0], z_recv.at[f, 0], (up, n)),
        ]
        for s, (side, _) in enumerate(sides):
            copies += [
                send(faces.at[f, s, pl.ds(0, 8)], from_c.at[f, s, 1], c_send.at[f, s, 1], c_recv.at[f, s, 1], (down, side)),
                send(faces.at[f, s, pl.ds(8, 8)], from_c.at[f, s, 0], c_send.at[f, s, 0], c_recv.at[f, s, 0], (up, side)),
            ]
        return copies

    def send_cycle(f):
        return [
            send(faces.at[f, s], from_a.at[f, s], a_send.at[f, s], a_recv.at[f, s], (w, side))
            for s, (side, _) in enumerate(sides)
        ]

    def whole_plane(f, i):
        value = slab(fields.at[f], i)
        row = value[0]
        for s in range(len(sides)):
            row = row + from_a[f, s, pl.ds(8 * POS[i], 8), :]
        if i in FACE:
            come = from_z[f, POS[i]].reshape(4, 8, 128)
            row = row + come[0]
            for s in range(len(sides)):
                row = row + from_c[f, s, POS[i]]
            return jnp.concatenate([row[None], value[1:] + come[1:]], axis=0)
        return jnp.concatenate([row[None], value[1:]], axis=0)

    def wait_all(copies):
        for copy in copies:
            copy.wait_recv()

    def weighted(one, two):
        total = None
        for i in range(8):
            product = one(i) * two(i)
            term = (product[1] + product[2]) + product[3] + product[0] * 0.5
            if i in (0, 7):
                term = term * 0.5
            total = term if total is None else total + term
        shared = ((node == 0) & (radial > 0)) | ((node == 7) & (radial < 15))
        return jnp.where(shared, total * 0.5, total)

    def stack_rows(terms):
        out = jnp.zeros((8, 128), F32)
        for q, term in enumerate(terms):
            out = jnp.where(node == q, jnp.sum(term, axis=0, keepdims=True), out)
        return out

    counts = [len(partners) for partners in phases]

    def sum_start(r, p, value):
        part[r, p] = value
        at = sum(counts[:p])
        return [
            send(part.at[r, p], gathered.at[r, at + q], g_send.at[r, at + q], g_recv.at[r, at + q], device)
            for q, device in enumerate(phases[p])
        ]

    def sum_end(r, p, copies):
        at = sum(counts[:p])
        total = part[r, p]
        for q, copy in enumerate(copies):
            copy.wait_recv()
            total = total + gathered[r, at + q]
        return total

    def sum_rest(r, p, copies):
        total = sum_end(r, p, copies)
        for later in range(p + 1, len(phases)):
            total = sum_end(r, later, sum_start(r, later, total))
        return jnp.sum(total, axis=1, keepdims=True)

    center = (interval_high + interval_low) / 2.0
    half_width = (interval_high - interval_low) / 2.0
    sigma = center / half_width
    rhos = [1.0 / sigma]
    for _ in range(2):
        rhos.append(1.0 / (2.0 * sigma - rhos[-1]))

    assemble_own(0, 0, 32)
    for i in range(8):
        bound_fluxes(i)
    part_z = along_eight(h_z, ABS.T, 1)
    radial_apply(radial_in, ABS.T, 1, 0, 8)
    for i in FACE:
        bound_total(i, part_z)
    assemble_own(1, 0, 8)
    pl.semaphore_wait(barrier, len(greeted))
    pipe = send_pipe(1) + send_pipe(0)
    radial_apply(radial_in, ABS.T, 1, 8, 24)
    for i in INNER:
        bound_total(i, part_z)
    assemble_own(1, 8, 24)
    cycle = send_cycle(1) + send_cycle(0)
    for q in (3, 5):
        metric[q] = metric[q] * mirror

    def begin(i):
        inverse = 1.0 / whole_plane(1, i)
        load_plane = whole_plane(0, i)
        update = load_plane * inverse * (1.0 / center)
        put(binv, i, inverse)
        put(res, i, load_plane)
        put(zed, i, update)
        put(dee, i, update)

    wait_all(cycle)
    for i in INNER:
        begin(i)
    forward_inner()
    wait_all(pipe)
    for i in FACE:
        begin(i)

    def apply_then(f, update, between=None, last=None):
        energy = forward_face(f)
        assemble_own(f, 0, 8)
        pipe = send_pipe(f)
        energy = energy + forward_rest(f)
        assemble_own(f, 8, 24)
        cycle = send_cycle(f)
        after = between(energy) if between is not None else None
        wait_all(cycle)
        for i in INNER:
            update(i, whole_plane(f, i))
        forward_inner()
        wait_all(pipe)
        for i in FACE:
            update(i, whole_plane(f, i))
        return after

    def smoothed(source, step, i, plane):
        now, later = rhos[step], rhos[step + 1]
        return slab(dee, i) * (now * later) + slab(binv, i) * (slab(source, i) - plane) * (2.0 * later / half_width)

    def smooth(source, step):
        def update(i, plane):
            change = smoothed(source, step, i, plane)
            put(dee, i, change)
            put(zed, i, slab(zed, i) + change)

        return update

    apply_then(2, smooth(res, 0))
    apply_then(3, smooth(res, 1))

    def start_norm(energy):
        norm = weighted(lambda i: slab(res, i), lambda i: slab(zed, i))
        return sum_start(0, 0, stack_rows([norm, energy]))

    def restart(i, plane):
        put(image, i, plane)
        put(first, i, slab(zed, i))
        update = plane * slab(binv, i) * (1.0 / center)
        put(zed, i, update)
        put(dee, i, update)

    sums = apply_then(4, restart, start_norm)
    more = apply_then(5, smooth(image, 0), lambda energy: sum_start(0, 1, sum_end(0, 0, sums)))
    scalars = {}

    def finish_norm(energy):
        total = sum_rest(0, 1, more)
        scalars["norm"], scalars["energy"] = total[0:1], total[1:2]
        scalars["alpha"] = total[0:1] / total[1:2]

    def step_on(i, plane):
        end = slab(zed, i) + smoothed(image, 1, i, plane)
        put(res, i, slab(res, i) - scalars["alpha"] * slab(image, i))
        put(zed, i, slab(first, i) - scalars["alpha"] * end)

    apply_then(6, step_on, finish_norm)
    norm_0, energy_0, alpha_0 = scalars["norm"], scalars["energy"], scalars["alpha"]

    def read_back(value_of, planes):
        rows = []
        for i in planes:
            value = value_of(i)
            for j in range(8):
                keep = (lane < 64) if j < 4 else (lane >= 64)
                rows.append(jnp.where(keep, value[j if j < 4 else 7 - j], 0.0))
        full = jnp.stack(rows).reshape(64 * len(planes), 128)
        high = full.astype(jnp.bfloat16)
        low = (full - high.astype(F32)).astype(jnp.bfloat16)
        dims = (((1,), (1,)), ((), ()))
        return lax.dot_general(hot_both, high, dims, preferred_element_type=F32) + lax.dot_general(
            hot_both, low, dims, preferred_element_type=F32
        )

    energy = forward_face(7)
    assemble_own(7, 0, 8)
    pipe = send_pipe(7)
    energy = energy + forward_rest(7)
    norm = weighted(lambda i: slab(res, i), lambda i: slab(zed, i))
    cross = weighted(lambda i: slab(zed, i), lambda i: slab(image, i))
    sums = sum_start(1, 0, stack_rows([norm, cross, energy]))
    assemble_own(7, 8, 24)
    cycle = send_cycle(7)
    for q, ref in enumerate((first, zed)):
        read[q] = read_back(lambda i: slab(ref, i), range(8))
    totals = sum_end(1, 0, sums)
    for later in range(1, len(phases) - 1):
        totals = sum_end(1, later, sum_start(1, later, totals))
    sums = sum_start(1, len(phases) - 1, totals)
    for q, ref in enumerate((res, image)):
        read[2 + q] = read_back(lambda i: slab(ref, i), range(8))
    wait_all(cycle)
    middle = read_back(lambda i: whole_plane(7, i), range(2, 6))
    total = jnp.sum(sum_end(1, len(phases) - 1, sums), axis=1, keepdims=True)
    norm_1, cross_1, energy_1 = total[0:1], total[1:2], total[2:3]
    beta = norm_1 / norm_0
    alpha_1 = norm_1 / (energy_1 + 2.0 * beta * cross_1 + beta * beta * energy_0)
    solution_ref[...] = (alpha_0 + alpha_1 * beta) * read[0] + alpha_1 * read[1]
    residual = read[2] - (alpha_1 * beta) * read[3]
    residual_ref[:, 128:384] = residual[:, 128:384] - alpha_1 * middle
    wait_all(pipe)
    ends = read_back(lambda i: whole_plane(7, i), (0, 1, 6, 7))
    residual_ref[:, 0:128] = residual[:, 0:128] - alpha_1 * ends[:, 0:128]
    residual_ref[:, 384:512] = residual[:, 384:512] - alpha_1 * ends[:, 128:256]
    for copy in started:
        copy.wait_send()


def solution(mesh):
    n_wide, n_narrow = mesh.shape["wide"], mesh.shape["narrow"]
    sides = 1 if n_narrow == 2 else 2
    factors = wide_factors(n_wide)
    partners = n_narrow * factors[0] - 1 + sum(factor - 1 for factor in factors[1:])
    vmem = pltpu.VMEM
    block = vmem((256, 128), F32)
    dma = pltpu.SemaphoreType.DMA

    def local(load, geom, element_order):
        whole = pl.BlockSpec(memory_space=pltpu.VMEM)
        shape = jax.ShapeDtypeStruct(load.shape, F32)
        return pl.pallas_call(
            functools.partial(body, n_wide, n_narrow),
            out_shape=(shape, shape),
            in_specs=[pl.BlockSpec(memory_space=pltpu.HBM)] * 3,
            out_specs=(whole, whole),
            scratch_shapes=[
                vmem(load.shape, F32),
                vmem(geom.shape, geom.dtype),
                vmem(element_order.shape, jnp.int32),
                vmem((7, 256, 128), F32),
                block,
                block,
                block,
                block,
                block,
                block,
                vmem((FIELDS, 256, 128), F32),
                vmem((FIELDS, sides, 64, 128), F32),
                block,
                block,
                block,
                block,
                block,
                block,
                vmem((4, 64, 512), F32),
                vmem((2, len(factors), 8, 128), F32),
                vmem((FIELDS, 2, 32, 128), F32),
                vmem((FIELDS, sides, 64, 128), F32),
                vmem((FIELDS, sides, 2, 8, 128), F32),
                vmem((2, partners, 8, 128), F32),
                dma((FIELDS, 2)),
                dma((FIELDS, 2)),
                dma((FIELDS, sides)),
                dma((FIELDS, sides)),
                dma((FIELDS, sides, 2)),
                dma((FIELDS, sides, 2)),
                dma((2, partners)),
                dma((2, partners)),
                dma((3,)),
            ],
            compiler_params=pltpu.CompilerParams(
                collective_id=0, has_side_effects=True, vmem_limit_bytes=60 * 1024 * 1024
            ),
        )(load, geom, element_order)

    return jax.shard_map(
        local,
        mesh=mesh,
        in_specs=(
            P(("wide", "narrow"), None),
            P(None, ("wide", "narrow"), None),
            P("wide", "narrow", None),
        ),
        out_specs=(P(("wide", "narrow"), None), P(("wide", "narrow"), None)),
        check_vma=False,
    )
```

```python
import functools

import jax
import jax.numpy as jnp
import numpy as np
from jax import lax
from jax.experimental import pallas as pl
from jax.experimental.pallas import tpu as pltpu
from jax.sharding import PartitionSpec as P

MESH = pl.DeviceIdType.MESH
interval_low = 0.03
interval_high = 1.0
FIELDS = 8
F32 = jnp.float32


ORDER = [0, 7, 1, 6, 2, 5, 3, 4]
POS = [ORDER.index(i) for i in range(8)]
FACE = [0, 7]
INNER = [1, 6, 2, 5, 3, 4]


def legendre_seven(point):
    before = 1.0
    current = point
    for degree in range(1, 7):
        after = ((2.0 * degree + 1.0) * point * current - degree * before) / (degree + 1.0)
        before = current
        current = after
    return current


def gll_derivative():
    points = 8
    inner_nodes = [
        -0.8717401485096066,
        -0.5917001814331423,
        -0.2092992179024789,
        0.2092992179024789,
        0.5917001814331423,
        0.8717401485096066,
    ]
    nodes = [-1.0] + inner_nodes + [1.0]
    values_at = [legendre_seven(node) for node in nodes]
    matrix = np.zeros((points, points))
    for source in range(points):
        for target in range(points):
            if source != target:
                matrix[source, target] = values_at[source] / (
                    values_at[target] * (nodes[source] - nodes[target])
                )
    matrix[0, 0] = -(points - 1) * points / 4.0
    matrix[points - 1, points - 1] = (points - 1) * points / 4.0
    return matrix


DERIV = gll_derivative()
ABS = np.abs(DERIV)
ROW_TOTAL = ABS.sum(axis=1)


def halves(matrix):
    even = (matrix[:4, :4] + matrix[:4, :3:-1]) / 2.0
    odd = (matrix[:4, :4] - matrix[:4, :3:-1]) / 2.0
    return even, odd


def combine(row, terms):
    total = terms[0] * float(row[0])
    for factor, term in zip(row[1:], terms[1:]):
        total = total + term * float(factor)
    return total


def along_eight(values, matrix, parity):
    even, odd = halves(matrix)
    sums = [values[m] + values[7 - m] for m in range(4)]
    differences = [values[m] - values[7 - m] for m in range(4)]
    result = [None] * 8
    for i in range(4):
        e = combine(even[i], sums)
        o = combine(odd[i], differences)
        result[i] = e + o
        result[7 - i] = (e - o) if parity > 0 else (o - e)
    return result


def lane_roll(value, shift):
    shape = value.shape
    flat = value.reshape(-1, shape[-1])
    return pltpu.roll(flat, shift, 1).reshape(shape)


def along_mirrored(value, matrix, sign):
    even, odd = halves(matrix)
    other = lane_roll(value, 64)
    plus, minus = value + other, value - other
    sums, differences = (plus, minus) if sign > 0 else (minus, plus)
    rows = []
    for j in range(4):
        rows.append(
            combine(even[j], [sums[m] for m in range(4)])
            + combine(odd[j], [differences[m] for m in range(4)])
        )
    return jnp.stack(rows)


def wide_factors(count):
    factors = []
    while count > 1:
        for factor in (4, 3, 2, 5, 7):
            if count % factor == 0:
                break
        else:
            factor = count
        factors.append(factor)
        count //= factor
    return factors


def body(
    n_wide,
    n_narrow,
    load_hbm,
    geom_hbm,
    order_hbm,
    solution_ref,
    residual_ref,
    load_ref,
    geom_ref,
    order_ref,
    metric,
    radial_in,
    radial_out,
    part_fz,
    part_fa,
    part_fr,
    grad_z,
    fields,
    faces,
    far_plane,
    far_line,
    planes,
    from_planes,
    res,
    binv,
    zed,
    dee,
    image,
    first,
    read,
    part,
    from_z,
    from_a,
    from_c,
    gathered,
    z_send,
    z_recv,
    a_send,
    a_recv,
    c_send,
    c_recv,
    g_send,
    g_recv,
    in_sem,
    p_send,
    p_recv,
):
    fetches = [
        pltpu.make_async_copy(order_hbm, order_ref, in_sem.at[0]),
        pltpu.make_async_copy(load_hbm, load_ref, in_sem.at[1]),
        pltpu.make_async_copy(geom_hbm, geom_ref, in_sem.at[2]),
    ]
    for fetch in fetches:
        fetch.start()
    w = lax.axis_index("wide")
    n = lax.axis_index("narrow")
    odd_one = lax.rem(w, 2)
    near = lax.rem(w + n_wide + 1 - 2 * odd_one, n_wide)
    far = lax.rem(w + n_wide - 1 + 2 * odd_one, n_wide)
    if n_narrow == 2:
        sides = [(lax.rem(n + 1, 2), 0)]
    else:
        sides = [(lax.rem(n + 1, n_narrow), 1), (lax.rem(n + n_narrow - 1, n_narrow), 2)]

    phases = []
    stride = 1
    for number, factor in enumerate(wide_factors(n_wide)):
        place = lax.rem(w // stride, factor)
        base = w - place * stride
        partners = []
        for dn in range(n_narrow if number == 0 else 1):
            for dw in range(factor):
                if dn == 0 and dw == 0:
                    continue
                there = base + lax.rem(place + dw, factor) * stride
                partners.append((there, lax.rem(n + dn, n_narrow)))
        phases.append(partners)
        stride *= factor

    barrier = pltpu.get_barrier_semaphore()
    greeted = [(near, n), (far, n)]
    for side, _ in sides:
        greeted += [(near, side), (far, side), (w, side)]
    for partners in phases:
        greeted += partners
    for device in greeted:
        pl.semaphore_signal(barrier, inc=1, device_id=device, device_id_type=MESH)

    lane = lax.broadcasted_iota(jnp.int32, (8, 128), 1)
    node = lax.broadcasted_iota(jnp.int32, (8, 128), 0)
    radial = lane % 16
    lane_row = lax.broadcasted_iota(jnp.int32, (1, 128), 1)
    mirror = jnp.where(lane_row < 64, 1.0, -1.0).astype(F32)
    radial_row = lane_row % 16
    odd_row = (lane_row * 0 + odd_one) == 1
    pipe_mirror = jnp.where(odd_row, -1.0, 1.0).astype(F32)

    for fetch in fetches:
        fetch.wait()
    order = order_ref[0].astype(jnp.int32)
    order_twice = jnp.concatenate([order, order + 64], axis=1)
    hot_t = (lax.broadcasted_iota(jnp.int32, (128, 128), 0) == order_twice).astype(F32)
    hot = jnp.transpose(hot_t)
    hot_both = (hot[:64] + hot[64:]).astype(jnp.bfloat16)
    top, bottom = hot[:64], hot[64:]
    zero = jnp.zeros_like(top)
    into_low = jnp.concatenate(
        [jnp.concatenate([top, zero], axis=1), jnp.concatenate([zero, top], axis=1)], axis=0
    ).astype(jnp.bfloat16)
    into_high = jnp.concatenate(
        [jnp.concatenate([bottom, zero], axis=1), jnp.concatenate([zero, bottom], axis=1)], axis=0
    ).astype(jnp.bfloat16)

    def oriented(value):
        pairs = value.reshape(4, 2, 32, 128)
        swapped = jnp.stack([pairs[:, 1], pairs[:, 0]], axis=1).reshape(256, 128)
        return jnp.where(odd_row, swapped, value)

    def place_pair(one, two):
        turned = jnp.transpose(jnp.concatenate([one, two], axis=0)).astype(jnp.bfloat16)
        split = turned.reshape(8, 8, 8, 128)
        low = jnp.stack([split[i, j] for i in ORDER for j in range(4)]).reshape(256, 128)
        high = jnp.stack([split[i, 7 - j] for i in ORDER for j in range(4)]).reshape(256, 128)
        both = jnp.dot(low, into_low, preferred_element_type=F32)
        both = both + jnp.dot(high, into_high, preferred_element_type=F32)
        one, two = both[:, :128], both[:, 128:]
        return oriented(one), oriented(two)

    def rounded(value):
        return value.astype(jnp.bfloat16).astype(F32)

    load = load_ref[...]
    load_high = rounded(load)
    load_rest = load - load_high
    load_mid = rounded(load_rest)
    load_low = rounded(load_rest - load_mid)
    g = [geom_ref[q].astype(F32) for q in range(7)]
    for q in (0, 2, 4):
        metric[q], metric[q + 1] = place_pair(g[q], g[q + 1])
    metric[6], grid_high = place_pair(g[6], load_high)
    grid_mid, grid_low = place_pair(load_mid, load_low)
    fields[0] = grid_high + (grid_mid + grid_low)

    def slab(ref, i):
        return ref[pl.ds(32 * POS[i], 32), :].reshape(4, 8, 128)

    def put(ref, i, value):
        ref[pl.ds(32 * POS[i], 32), :] = value.reshape(32, 128)

    def radial_apply(source, matrix, parity, start=0, count=32):
        values = [source[pl.ds(8 * start + k, count, stride=8), :] for k in range(8)]
        result = along_eight(values, matrix, parity)
        for k in range(8):
            radial_out[pl.ds(8 * start + k, count, stride=8), :] = result[k]

    q_r = jnp.full((8, 128), float(ROW_TOTAL[0]), F32)
    for k in range(1, 4):
        q_r = jnp.where((node == k) | (node == 7 - k), float(ROW_TOTAL[k]), q_r)
    h_z, part_a = [None] * 8, [None] * 8

    def by_cycle(value):
        return jnp.stack([value[j] * float(ROW_TOTAL[j]) for j in range(4)])

    def bound_fluxes(i):
        a = [jnp.abs(slab(metric.at[q], i)) for q in range(6)]
        q_z = float(ROW_TOTAL[i])
        h_z[i] = a[0] * q_z + by_cycle(a[3]) + a[4] * q_r
        part_a[i] = along_mirrored(a[3] * q_z + by_cycle(a[1]) + a[5] * q_r, ABS.T, 1)
        put(radial_in, i, a[4] * q_z + by_cycle(a[5]) + a[2] * q_r)

    def bound_total(i, part_z):
        put(fields.at[1], i, part_z[i] + part_a[i] + slab(radial_out, i) + jnp.abs(slab(metric.at[6], i)))

    even, odd = halves(DERIV)
    even_t, odd_t = halves(DERIV.T)

    def forward_inner():
        radial_apply(zed, DERIV, -1, 8, 24)
        for i in INNER:
            grad_a = along_mirrored(slab(zed, i), DERIV, 1)
            grad_r = slab(radial_out, i)
            put(part_fz, i, slab(metric.at[3], i) * grad_a + slab(metric.at[4], i) * grad_r)
            put(part_fa, i, slab(metric.at[1], i) * grad_a + slab(metric.at[5], i) * grad_r)
            put(part_fr, i, slab(metric.at[5], i) * grad_a + slab(metric.at[2], i) * grad_r)
        for j in range(4):
            v = [tile(zed, i, j) for i in range(1, 7)]
            sums = [v[m] + v[5 - m] for m in range(3)]
            differences = [v[m] - v[5 - m] for m in range(3)]
            for i in range(4):
                e, o = combine(even[i][1:], sums), combine(odd[i][1:], differences)
                put_tile(grad_z, i, j, e + o)
                put_tile(grad_z, 7 - i, j, o - e)

    def tile(ref, i, j):
        return ref[pl.ds(32 * POS[i] + 8 * j, 8), :]

    def put_tile(ref, i, j, value):
        ref[pl.ds(32 * POS[i] + 8 * j, 8), :] = value

    def add_slopes(column, plane):
        for i in range(8):
            put(grad_z, i, slab(grad_z, i) + plane * float(DERIV[i][column]))

    def forward_far(f):
        radial_apply(zed, DERIV, -1, 4, 4)
        plane = slab(zed, 7)
        grad_a = along_mirrored(plane, DERIV, 1)
        grad_r = slab(radial_out, 7)
        add_slopes(7, plane)
        put(part_fz, 7, slab(metric.at[3], 7) * grad_a + slab(metric.at[4], 7) * grad_r)
        put(part_fa, 7, slab(metric.at[1], 7) * grad_a + slab(metric.at[5], 7) * grad_r)
        put(part_fr, 7, slab(metric.at[5], 7) * grad_a + slab(metric.at[2], 7) * grad_r)
        slope = slab(grad_z, 0)
        put(radial_in, 0, slab(metric.at[4], 0) * slope)
        radial_apply(radial_in, DERIV.T, -1, 0, 4)
        total = along_mirrored(slab(metric.at[3], 0) * slope, DERIV.T, -1) + slab(metric.at[0], 0) * slope * float(DERIV[0][0])
        for i in range(1, 8):
            flux = slab(part_fz, i) + slab(metric.at[0], i) * slab(grad_z, i)
            total = total + flux * float(DERIV[i][0])
        total = total + slab(radial_out, 0)
        far_plane[f] = total.reshape(32, 128)

        def keep(at, s, message):
            far_line[f, s] = message

        assemble_at(far_plane.at[f], 0, 4, keep)
        copies = [send(far_plane.at[f], from_z.at[f, 0], z_send.at[f, 0], z_recv.at[f, 0], (far, n))]
        for s, (side, _) in enumerate(sides):
            copies.append(send(far_line.at[f, s], from_c.at[f, s, 0], c_send.at[f, s, 0], c_recv.at[f, s, 0], (far, side)))
        return total, copies

    def forward_face(f, far_part):
        radial_apply(zed, DERIV, -1, 0, 4)
        plane = slab(zed, 0)
        grad_a = along_mirrored(plane, DERIV, 1)
        grad_r = slab(radial_out, 0)
        add_slopes(0, plane)
        c = [planes[q].reshape(4, 8, 128) for q in range(6)]
        put(radial_in, 0, c[2] * plane + c[5] * grad_a + c[4] * grad_r)
        flux_a = c[1] * plane + c[3] * grad_a + c[5] * grad_r
        put(part_fz, 0, slab(metric.at[3], 0) * grad_a + slab(metric.at[4], 0) * grad_r)
        near_slope = slab(grad_z, 7)
        put(radial_in, 7, slab(part_fr, 7) + slab(metric.at[4], 7) * near_slope)
        radial_apply(radial_in, DERIV.T, -1, 0, 8)
        own = c[0] * plane + c[1] * grad_a + c[2] * grad_r + along_mirrored(flux_a, DERIV.T, -1) + slab(radial_out, 0)
        total = along_mirrored(slab(part_fa, 7) + slab(metric.at[3], 7) * near_slope, DERIV.T, -1)
        total = total + slab(metric.at[6], 7) * slab(zed, 7) + slab(radial_out, 7)
        for i in range(8):
            flux = slab(part_fz, i) + slab(metric.at[0], i) * slab(grad_z, i)
            put(part_fz, i, flux)
            total = total + flux * float(DERIV[i][7])
        put(fields.at[f], 0, own + far_part)
        put(fields.at[f], 7, total)
        return jnp.sum((far_part + own * 0.5) * plane + total * slab(zed, 7), axis=0)

    def forward_rest(f):
        energy = jnp.zeros((8, 128), F32)
        for i in INNER:
            slope = slab(grad_z, i)
            flux_a = slab(part_fa, i) + slab(metric.at[3], i) * slope
            put(radial_in, i, slab(part_fr, i) + slab(metric.at[4], i) * slope)
            put(part_fa, i, along_mirrored(flux_a, DERIV.T, -1) + slab(metric.at[6], i) * slab(zed, i))
        radial_apply(radial_in, DERIV.T, -1, 8, 24)
        for j in range(4):
            flux_z = [tile(part_fz, i, j) for i in range(8)]
            sums = [flux_z[m] + flux_z[7 - m] for m in range(4)]
            differences = [flux_z[m] - flux_z[7 - m] for m in range(4)]
            for i in range(1, 4):
                e, o = combine(even_t[i], sums), combine(odd_t[i], differences)
                for node_i, piece in ((i, e + o), (7 - i, o - e)):
                    total = piece + tile(part_fa, node_i, j) + tile(radial_out, node_i, j)
                    put_tile(fields.at[f], node_i, j, total)
                    energy = energy + total * tile(zed, node_i, j)
        return energy

    def assemble_own(f, start, count):
        def keep(at, s, message):
            faces[f, s, pl.ds(8 * at, 8), :] = message

        assemble_at(fields.at[f], start, count, keep)

    def assemble_at(ref, start, count, keep):
        low = pl.ds(8 * start, count, stride=8)
        high = pl.ds(8 * start + 7, count, stride=8)
        inner, outer = ref[low, :], ref[high, :]
        ref[low, :] = inner + jnp.where(radial_row > 0, pltpu.roll(outer, 1, 1), 0.0)
        ref[high, :] = outer + jnp.where(radial_row < 15, pltpu.roll(inner, 127, 1), 0.0)
        for at in range(start // 4, (start + count) // 4):
            row = ref[pl.ds(32 * at, 8), :]
            below = pltpu.roll(row, 16, 1)
            above = pltpu.roll(row, 112, 1)
            for s, (_, kind) in enumerate(sides):
                message = jnp.zeros_like(row)
                if kind in (0, 1):
                    message = jnp.where(lane < 16, below, message)
                if kind in (0, 2):
                    message = jnp.where(lane >= 112, above, message)
                keep(at, s, message)
            inside = jnp.where(lane < 64, pltpu.roll(row, 80, 1), pltpu.roll(row, 48, 1))
            ref[pl.ds(32 * at, 8), :] = row + jnp.where((lane >= 16) & (lane < 112), inside, 0.0)

    started = []

    def send(src, dst, send_sem, recv_sem, device):
        copy = pltpu.make_async_remote_copy(
            src_ref=src, dst_ref=dst, send_sem=send_sem, recv_sem=recv_sem, device_id=device, device_id_type=MESH
        )
        copy.start()
        started.append(copy)
        return copy

    def send_face(f, face, device):
        rows, line = pl.ds(32 * face, 32), pl.ds(8 * face, 8)
        copies = [
            send(fields.at[f, rows], from_z.at[f, face], z_send.at[f, face], z_recv.at[f, face], (device, n))
        ]
        for s, (side, _) in enumerate(sides):
            copies.append(
                send(faces.at[f, s, line], from_c.at[f, s, face], c_send.at[f, s, face], c_recv.at[f, s, face], (device, side))
            )
        return copies

    def send_cycle(f):
        return [
            send(faces.at[f, s], from_a.at[f, s], a_send.at[f, s], a_recv.at[f, s], (w, side))
            for s, (side, _) in enumerate(sides)
        ]

    def whole_plane(f, i):
        value = slab(fields.at[f], i)
        row = value[0]
        for s in range(len(sides)):
            row = row + from_a[f, s, pl.ds(8 * POS[i], 8), :]
        if i in FACE:
            come = from_z[f, POS[i]].reshape(4, 8, 128)
            row = row + come[0]
            for s in range(len(sides)):
                row = row + from_c[f, s, POS[i]]
            return jnp.concatenate([row[None], value[1:] + come[1:]], axis=0)
        return jnp.concatenate([row[None], value[1:]], axis=0)

    def wait_all(copies):
        for copy in copies:
            copy.wait_recv()

    def weighted(one, two):
        total = None
        for i in range(8):
            product = one(i) * two(i)
            term = (product[1] + product[2]) + product[3] + product[0] * 0.5
            if i in (0, 7):
                term = term * 0.5
            total = term if total is None else total + term
        shared = ((node == 0) & (radial > 0)) | ((node == 7) & (radial < 15))
        return jnp.where(shared, total * 0.5, total)

    def stack_rows(terms):
        out = jnp.zeros((8, 128), F32)
        for q, term in enumerate(terms):
            out = jnp.where(node == q, jnp.sum(term, axis=0, keepdims=True), out)
        return out

    counts = [len(partners) for partners in phases]

    def sum_start(r, p, value):
        part[r, p] = value
        at = sum(counts[:p])
        return [
            send(part.at[r, p], gathered.at[r, at + q], g_send.at[r, at + q], g_recv.at[r, at + q], device)
            for q, device in enumerate(phases[p])
        ]

    def sum_end(r, p, copies):
        at = sum(counts[:p])
        total = part[r, p]
        for q, copy in enumerate(copies):
            copy.wait_recv()
            total = total + gathered[r, at + q]
        return total

    def sum_rest(r, p, copies):
        total = sum_end(r, p, copies)
        for later in range(p + 1, len(phases)):
            total = sum_end(r, later, sum_start(r, later, total))
        return jnp.sum(total, axis=1, keepdims=True)

    center = (interval_high + interval_low) / 2.0
    half_width = (interval_high - interval_low) / 2.0
    sigma = center / half_width
    rhos = [1.0 / sigma]
    for _ in range(2):
        rhos.append(1.0 / (2.0 * sigma - rhos[-1]))

    assemble_own(0, 0, 32)
    for i in range(8):
        bound_fluxes(i)
    part_z = along_eight(h_z, ABS.T, 1)
    radial_apply(radial_in, ABS.T, 1, 0, 8)
    for i in FACE:
        bound_total(i, part_z)
    assemble_own(1, 0, 8)
    pl.semaphore_wait(barrier, len(greeted))
    from_far = send_face(1, 0, far) + send_face(0, 0, far)
    from_near = send_face(1, 1, near) + send_face(0, 1, near)
    corner = float(DERIV[0][0])
    own = slab(metric.at[6], 0)
    for i in range(8):
        own = own + slab(metric.at[0], i) * float(DERIV[i][0] ** 2)
    for q, plane in enumerate(
        (
            own,
            slab(metric.at[3], 0) * (mirror * pipe_mirror * corner),
            slab(metric.at[4], 0) * (pipe_mirror * corner),
            slab(metric.at[1], 0),
            slab(metric.at[2], 0),
            slab(metric.at[5], 0) * mirror,
        )
    ):
        planes[q] = plane.reshape(32, 128)
    planes_copy = pltpu.make_async_remote_copy(
        src_ref=planes,
        dst_ref=from_planes,
        send_sem=p_send.at[0],
        recv_sem=p_recv.at[0],
        device_id=(far, n),
        device_id_type=MESH,
    )
    planes_copy.start()
    radial_apply(radial_in, ABS.T, 1, 8, 24)
    for i in INNER:
        bound_total(i, part_z)
    assemble_own(1, 8, 24)
    cycle = send_cycle(1) + send_cycle(0)
    metric[3] = metric[3] * (mirror * pipe_mirror)
    metric[4] = metric[4] * pipe_mirror
    metric[5] = metric[5] * mirror

    def begin(i):
        inverse = 1.0 / whole_plane(1, i)
        load_plane = whole_plane(0, i)
        update = load_plane * inverse * (1.0 / center)
        put(binv, i, inverse)
        put(res, i, load_plane)
        put(zed, i, update)
        put(dee, i, update)

    wait_all(cycle)
    for i in INNER:
        begin(i)
    forward_inner()
    wait_all(from_near)
    begin(7)
    pending = [from_far, lambda: begin(0)]

    def both_faces(f):
        far_part, copies = forward_far(f)
        wait_all(pending[0])
        pending[1]()
        if f == 2:
            planes_copy.wait()
            planes[...] = planes[...] + from_planes[...]
        energy = forward_face(f, far_part)
        assemble_own(f, 0, 8)
        return energy, copies, send_face(f, 1, near)

    def apply_then(f, update, between=None):
        energy, from_far, from_near = both_faces(f)
        energy = energy + forward_rest(f)
        assemble_own(f, 8, 24)
        cycle = send_cycle(f)
        after = between(energy) if between is not None else None
        wait_all(cycle)
        for i in INNER:
            update(i, whole_plane(f, i))
        forward_inner()
        wait_all(from_near)
        update(7, whole_plane(f, 7))
        pending[:] = [from_far, lambda: update(0, whole_plane(f, 0))]
        return after

    def smoothed(source, step, i, plane):
        now, later = rhos[step], rhos[step + 1]
        return slab(dee, i) * (now * later) + slab(binv, i) * (slab(source, i) - plane) * (2.0 * later / half_width)

    def smooth(source, step):
        def update(i, plane):
            change = smoothed(source, step, i, plane)
            put(dee, i, change)
            put(zed, i, slab(zed, i) + change)

        return update

    apply_then(2, smooth(res, 0))
    apply_then(3, smooth(res, 1))

    def start_norm(energy):
        norm = weighted(lambda i: slab(res, i), lambda i: slab(zed, i))
        return sum_start(0, 0, stack_rows([norm, energy]))

    def restart(i, plane):
        put(image, i, plane)
        put(first, i, slab(zed, i))
        update = plane * slab(binv, i) * (1.0 / center)
        put(zed, i, update)
        put(dee, i, update)

    sums = apply_then(4, restart, start_norm)
    more = apply_then(5, smooth(image, 0), lambda energy: sum_start(0, 1, sum_end(0, 0, sums)))
    scalars = {}

    def finish_norm(energy):
        total = sum_rest(0, 1, more)
        scalars["norm"], scalars["energy"] = total[0:1], total[1:2]
        scalars["alpha"] = total[0:1] / total[1:2]

    def step_on(i, plane):
        end = slab(zed, i) + smoothed(image, 1, i, plane)
        put(res, i, slab(res, i) - scalars["alpha"] * slab(image, i))
        put(zed, i, slab(first, i) - scalars["alpha"] * end)

    apply_then(6, step_on, finish_norm)
    norm_0, energy_0, alpha_0 = scalars["norm"], scalars["energy"], scalars["alpha"]

    def read_back(value_of, chosen):
        rows = []
        for i in chosen:
            value = jnp.where(odd_row, value_of(7 - i), value_of(i))
            for j in range(8):
                keep = (lane < 64) if j < 4 else (lane >= 64)
                rows.append(jnp.where(keep, value[j if j < 4 else 7 - j], 0.0))
        full = jnp.stack(rows).reshape(64 * len(chosen), 128)
        high = full.astype(jnp.bfloat16)
        low = (full - high.astype(F32)).astype(jnp.bfloat16)
        dims = (((1,), (1,)), ((), ()))
        return lax.dot_general(hot_both, high, dims, preferred_element_type=F32) + lax.dot_general(
            hot_both, low, dims, preferred_element_type=F32
        )

    energy, from_far, from_near = both_faces(7)
    energy = energy + forward_rest(7)
    norm = weighted(lambda i: slab(res, i), lambda i: slab(zed, i))
    cross = weighted(lambda i: slab(zed, i), lambda i: slab(image, i))
    sums = sum_start(1, 0, stack_rows([norm, cross, energy]))
    assemble_own(7, 8, 24)
    cycle = send_cycle(7)
    for q, ref in enumerate((first, zed)):
        read[q] = read_back(lambda i: slab(ref, i), range(8))
    totals = sum_end(1, 0, sums)
    for later in range(1, len(phases) - 1):
        totals = sum_end(1, later, sum_start(1, later, totals))
    sums = sum_start(1, len(phases) - 1, totals)
    for q, ref in enumerate((res, image)):
        read[2 + q] = read_back(lambda i: slab(ref, i), range(8))
    wait_all(cycle)
    middle = read_back(lambda i: whole_plane(7, i), range(2, 6))
    total = jnp.sum(sum_end(1, len(phases) - 1, sums), axis=1, keepdims=True)
    norm_1, cross_1, energy_1 = total[0:1], total[1:2], total[2:3]
    beta = norm_1 / norm_0
    alpha_1 = norm_1 / (energy_1 + 2.0 * beta * cross_1 + beta * beta * energy_0)
    solution_ref[...] = (alpha_0 + alpha_1 * beta) * read[0] + alpha_1 * read[1]
    residual = read[2] - (alpha_1 * beta) * read[3]
    residual_ref[:, 128:384] = residual[:, 128:384] - alpha_1 * middle
    wait_all(from_near)
    wait_all(from_far)
    ends = read_back(lambda i: whole_plane(7, i), (0, 1, 6, 7))
    residual_ref[:, 0:128] = residual[:, 0:128] - alpha_1 * ends[:, 0:128]
    residual_ref[:, 384:512] = residual[:, 384:512] - alpha_1 * ends[:, 128:256]
    for copy in started:
        copy.wait_send()


def solution(mesh):
    n_wide, n_narrow = mesh.shape["wide"], mesh.shape["narrow"]
    sides = 1 if n_narrow == 2 else 2
    factors = wide_factors(n_wide)
    partners = n_narrow * factors[0] - 1 + sum(factor - 1 for factor in factors[1:])
    vmem = pltpu.VMEM
    block = vmem((256, 128), F32)
    dma = pltpu.SemaphoreType.DMA

    def local(load, geom, element_order):
        whole = pl.BlockSpec(memory_space=pltpu.VMEM)
        shape = jax.ShapeDtypeStruct(load.shape, F32)
        return pl.pallas_call(
            functools.partial(body, n_wide, n_narrow),
            out_shape=(shape, shape),
            in_specs=[pl.BlockSpec(memory_space=pltpu.HBM)] * 3,
            out_specs=(whole, whole),
            scratch_shapes=[
                vmem(load.shape, F32),
                vmem(geom.shape, geom.dtype),
                vmem(element_order.shape, jnp.int32),
                vmem((7, 256, 128), F32),
                block,
                block,
                block,
                block,
                block,
                block,
                vmem((FIELDS, 256, 128), F32),
                vmem((FIELDS, sides, 64, 128), F32),
                vmem((FIELDS, 32, 128), F32),
                vmem((FIELDS, sides, 8, 128), F32),
                vmem((6, 32, 128), F32),
                vmem((6, 32, 128), F32),
                block,
                block,
                block,
                block,
                block,
                block,
                vmem((4, 64, 512), F32),
                vmem((2, len(factors), 8, 128), F32),
                vmem((FIELDS, 2, 32, 128), F32),
                vmem((FIELDS, sides, 64, 128), F32),
                vmem((FIELDS, sides, 2, 8, 128), F32),
                vmem((2, partners, 8, 128), F32),
                dma((FIELDS, 2)),
                dma((FIELDS, 2)),
                dma((FIELDS, sides)),
                dma((FIELDS, sides)),
                dma((FIELDS, sides, 2)),
                dma((FIELDS, sides, 2)),
                dma((2, partners)),
                dma((2, partners)),
                dma((3,)),
                dma((1,)),
                dma((1,)),
            ],
            compiler_params=pltpu.CompilerParams(
                collective_id=0, has_side_effects=True, vmem_limit_bytes=60 * 1024 * 1024
            ),
        )(load, geom, element_order)

    return jax.shard_map(
        local,
        mesh=mesh,
        in_specs=(
            P(("wide", "narrow"), None),
            P(None, ("wide", "narrow"), None),
            P("wide", "narrow", None),
        ),
        out_specs=(P(("wide", "narrow"), None), P(("wide", "narrow"), None)),
        check_vma=False,
    )
```

```python
import functools

import jax
import jax.numpy as jnp
import numpy as np
from jax import lax
from jax.experimental import pallas as pl
from jax.experimental.pallas import tpu as pltpu
from jax.sharding import PartitionSpec as P

MESH = pl.DeviceIdType.MESH
interval_low = 0.03
interval_high = 1.0
FIELDS = 8
F32 = jnp.float32


ORDER = [0, 7, 1, 6, 2, 5, 3, 4]
POS = [ORDER.index(i) for i in range(8)]
FACE = [0, 7]
INNER = [1, 6, 2, 5, 3, 4]


def legendre_seven(point):
    before = 1.0
    current = point
    for degree in range(1, 7):
        after = ((2.0 * degree + 1.0) * point * current - degree * before) / (degree + 1.0)
        before = current
        current = after
    return current


def gll_derivative():
    points = 8
    inner_nodes = [
        -0.8717401485096066,
        -0.5917001814331423,
        -0.2092992179024789,
        0.2092992179024789,
        0.5917001814331423,
        0.8717401485096066,
    ]
    nodes = [-1.0] + inner_nodes + [1.0]
    values_at = [legendre_seven(node) for node in nodes]
    matrix = np.zeros((points, points))
    for source in range(points):
        for target in range(points):
            if source != target:
                matrix[source, target] = values_at[source] / (
                    values_at[target] * (nodes[source] - nodes[target])
                )
    matrix[0, 0] = -(points - 1) * points / 4.0
    matrix[points - 1, points - 1] = (points - 1) * points / 4.0
    return matrix


DERIV = gll_derivative()
ABS = np.abs(DERIV)
ROW_TOTAL = ABS.sum(axis=1)


def halves(matrix):
    even = (matrix[:4, :4] + matrix[:4, :3:-1]) / 2.0
    odd = (matrix[:4, :4] - matrix[:4, :3:-1]) / 2.0
    return even, odd


def combine(row, terms):
    total = terms[0] * float(row[0])
    for factor, term in zip(row[1:], terms[1:]):
        total = total + term * float(factor)
    return total


def along_eight(values, matrix, parity):
    even, odd = halves(matrix)
    sums = [values[m] + values[7 - m] for m in range(4)]
    differences = [values[m] - values[7 - m] for m in range(4)]
    result = [None] * 8
    for i in range(4):
        e = combine(even[i], sums)
        o = combine(odd[i], differences)
        result[i] = e + o
        result[7 - i] = (e - o) if parity > 0 else (o - e)
    return result


def lane_roll(value, shift):
    shape = value.shape
    flat = value.reshape(-1, shape[-1])
    return pltpu.roll(flat, shift, 1).reshape(shape)


def along_mirrored(value, matrix, sign):
    even, odd = halves(matrix)
    other = lane_roll(value, 64)
    plus, minus = value + other, value - other
    sums, differences = (plus, minus) if sign > 0 else (minus, plus)
    rows = []
    for j in range(4):
        rows.append(
            combine(even[j], [sums[m] for m in range(4)])
            + combine(odd[j], [differences[m] for m in range(4)])
        )
    return jnp.stack(rows)


def wide_factors(count):
    factors = []
    while count > 1:
        for factor in (4, 3, 2, 5, 7):
            if count % factor == 0:
                break
        else:
            factor = count
        factors.append(factor)
        count //= factor
    return factors


def body(
    n_wide,
    n_narrow,
    load_hbm,
    geom_hbm,
    order_hbm,
    solution_ref,
    residual_ref,
    load_ref,
    geom_ref,
    order_ref,
    metric,
    radial_in,
    radial_out,
    part_fz,
    part_fa,
    part_fr,
    grad_z,
    fields,
    faces,
    far_plane,
    far_line,
    planes,
    from_planes,
    res,
    binv,
    zed,
    dee,
    image,
    first,
    read,
    part,
    from_z,
    from_a,
    from_c,
    gathered,
    z_send,
    z_recv,
    a_send,
    a_recv,
    c_send,
    c_recv,
    g_send,
    g_recv,
    in_sem,
    p_send,
    p_recv,
):
    fetches = [
        pltpu.make_async_copy(order_hbm, order_ref, in_sem.at[0]),
        pltpu.make_async_copy(load_hbm, load_ref, in_sem.at[1]),
        pltpu.make_async_copy(geom_hbm, geom_ref, in_sem.at[2]),
    ]
    for fetch in fetches:
        fetch.start()
    w = lax.axis_index("wide")
    n = lax.axis_index("narrow")
    odd_one = lax.rem(w, 2)
    near = lax.rem(w + n_wide + 1 - 2 * odd_one, n_wide)
    far = lax.rem(w + n_wide - 1 + 2 * odd_one, n_wide)
    if n_narrow == 2:
        sides = [(lax.rem(n + 1, 2), 0)]
    else:
        sides = [(lax.rem(n + 1, n_narrow), 1), (lax.rem(n + n_narrow - 1, n_narrow), 2)]

    phases = []
    stride = 1
    for number, factor in enumerate(wide_factors(n_wide)):
        place = lax.rem(w // stride, factor)
        base = w - place * stride
        partners = []
        for dn in range(n_narrow if number == 0 else 1):
            for dw in range(factor):
                if dn == 0 and dw == 0:
                    continue
                there = base + lax.rem(place + dw, factor) * stride
                partners.append((there, lax.rem(n + dn, n_narrow)))
        phases.append(partners)
        stride *= factor

    barrier = pltpu.get_barrier_semaphore()
    greeted = [(near, n), (far, n)]
    for side, _ in sides:
        greeted += [(near, side), (far, side), (w, side)]
    for partners in phases:
        greeted += partners
    for device in greeted:
        pl.semaphore_signal(barrier, inc=1, device_id=device, device_id_type=MESH)

    lane = lax.broadcasted_iota(jnp.int32, (8, 128), 1)
    node = lax.broadcasted_iota(jnp.int32, (8, 128), 0)
    radial = lane % 16
    lane_row = lax.broadcasted_iota(jnp.int32, (1, 128), 1)
    mirror = jnp.where(lane_row < 64, 1.0, -1.0).astype(F32)
    radial_row = lane_row % 16
    odd_row = (lane_row * 0 + odd_one) == 1
    pipe_mirror = jnp.where(odd_row, -1.0, 1.0).astype(F32)

    fetches[0].wait()
    fetches[1].wait()
    order = order_ref[0].astype(jnp.int32)
    order_twice = jnp.concatenate([order, order + 64], axis=1)
    hot_t = (lax.broadcasted_iota(jnp.int32, (128, 128), 0) == order_twice).astype(F32)
    hot = jnp.transpose(hot_t)
    hot_both = (hot[:64] + hot[64:]).astype(jnp.bfloat16)
    top, bottom = hot[:64], hot[64:]
    zero = jnp.zeros_like(top)
    into_low = jnp.concatenate(
        [jnp.concatenate([top, zero], axis=1), jnp.concatenate([zero, top], axis=1)], axis=0
    ).astype(jnp.bfloat16)
    into_high = jnp.concatenate(
        [jnp.concatenate([bottom, zero], axis=1), jnp.concatenate([zero, bottom], axis=1)], axis=0
    ).astype(jnp.bfloat16)

    def oriented(value):
        pairs = value.reshape(4, 2, 32, 128)
        swapped = jnp.stack([pairs[:, 1], pairs[:, 0]], axis=1).reshape(256, 128)
        return jnp.where(odd_row, swapped, value)

    def place_pair(one, two):
        turned = jnp.transpose(jnp.concatenate([one, two], axis=0)).astype(F32)
        split = turned.reshape(8, 8, 8, 128)
        low = jnp.stack([split[i, j] for i in ORDER for j in range(4)]).reshape(256, 128).astype(jnp.bfloat16)
        high = jnp.stack([split[i, 7 - j] for i in ORDER for j in range(4)]).reshape(256, 128).astype(jnp.bfloat16)
        both = jnp.dot(low, into_low, preferred_element_type=F32)
        both = both + jnp.dot(high, into_high, preferred_element_type=F32)
        one, two = both[:, :128], both[:, 128:]
        return oriented(one), oriented(two)

    def rounded(value):
        return value.astype(jnp.bfloat16)

    load = load_ref[...]
    load_high = rounded(load)
    load_rest = load - load_high.astype(F32)
    load_mid = rounded(load_rest)
    load_low = rounded(load_rest - load_mid.astype(F32))
    fetches[2].wait()
    g = [geom_ref[q] for q in range(7)]
    for q in (0, 2, 4):
        metric[q], metric[q + 1] = place_pair(g[q], g[q + 1])
    metric[6], grid_high = place_pair(g[6], load_high)
    grid_mid, grid_low = place_pair(load_mid, load_low)
    fields[0] = grid_high + (grid_mid + grid_low)

    def slab(ref, i):
        return ref[pl.ds(32 * POS[i], 32), :].reshape(4, 8, 128)

    def put(ref, i, value):
        ref[pl.ds(32 * POS[i], 32), :] = value.reshape(32, 128)

    def radial_apply(source, matrix, parity, start=0, count=32):
        values = [source[pl.ds(8 * start + k, count, stride=8), :] for k in range(8)]
        result = along_eight(values, matrix, parity)
        for k in range(8):
            radial_out[pl.ds(8 * start + k, count, stride=8), :] = result[k]

    q_r = jnp.full((8, 128), float(ROW_TOTAL[0]), F32)
    for k in range(1, 4):
        q_r = jnp.where((node == k) | (node == 7 - k), float(ROW_TOTAL[k]), q_r)
    h_z, part_a = [None] * 8, [None] * 8

    def by_cycle(value):
        return jnp.stack([value[j] * float(ROW_TOTAL[j]) for j in range(4)])

    def bound_fluxes(i):
        a = [jnp.abs(slab(metric.at[q], i)) for q in range(6)]
        q_z = float(ROW_TOTAL[i])
        h_z[i] = a[0] * q_z + by_cycle(a[3]) + a[4] * q_r
        part_a[i] = along_mirrored(a[3] * q_z + by_cycle(a[1]) + a[5] * q_r, ABS.T, 1)
        put(radial_in, i, a[4] * q_z + by_cycle(a[5]) + a[2] * q_r)

    def bound_total(i, part_z):
        put(fields.at[1], i, part_z[i] + part_a[i] + slab(radial_out, i) + jnp.abs(slab(metric.at[6], i)))

    even, odd = halves(DERIV)
    even_t, odd_t = halves(DERIV.T)

    def forward_inner():
        radial_apply(zed, DERIV, -1, 8, 24)
        for i in INNER:
            grad_a = along_mirrored(slab(zed, i), DERIV, 1)
            grad_r = slab(radial_out, i)
            put(part_fz, i, slab(metric.at[3], i) * grad_a + slab(metric.at[4], i) * grad_r)
            put(part_fa, i, slab(metric.at[1], i) * grad_a + slab(metric.at[5], i) * grad_r)
            put(part_fr, i, slab(metric.at[5], i) * grad_a + slab(metric.at[2], i) * grad_r)
        for j in range(4):
            v = [tile(zed, i, j) for i in range(1, 7)]
            sums = [v[m] + v[5 - m] for m in range(3)]
            differences = [v[m] - v[5 - m] for m in range(3)]
            for i in range(4):
                e, o = combine(even[i][1:], sums), combine(odd[i][1:], differences)
                put_tile(grad_z, i, j, e + o)
                put_tile(grad_z, 7 - i, j, o - e)

    def tile(ref, i, j):
        return ref[pl.ds(32 * POS[i] + 8 * j, 8), :]

    def put_tile(ref, i, j, value):
        ref[pl.ds(32 * POS[i] + 8 * j, 8), :] = value

    def add_slopes(column, plane):
        for i in range(8):
            put(grad_z, i, slab(grad_z, i) + plane * float(DERIV[i][column]))

    def forward_far(f):
        radial_apply(zed, DERIV, -1, 4, 4)
        plane = slab(zed, 7)
        grad_a = along_mirrored(plane, DERIV, 1)
        grad_r = slab(radial_out, 7)
        add_slopes(7, plane)
        put(part_fz, 7, slab(metric.at[3], 7) * grad_a + slab(metric.at[4], 7) * grad_r)
        put(part_fa, 7, slab(metric.at[1], 7) * grad_a + slab(metric.at[5], 7) * grad_r)
        put(part_fr, 7, slab(metric.at[5], 7) * grad_a + slab(metric.at[2], 7) * grad_r)
        slope = slab(grad_z, 0)
        put(radial_in, 0, slab(metric.at[4], 0) * slope)
        radial_apply(radial_in, DERIV.T, -1, 0, 4)
        total = along_mirrored(slab(metric.at[3], 0) * slope, DERIV.T, -1) + slab(metric.at[0], 0) * slope * float(DERIV[0][0])
        for i in range(1, 8):
            flux = slab(part_fz, i) + slab(metric.at[0], i) * slab(grad_z, i)
            total = total + flux * float(DERIV[i][0])
        total = total + slab(radial_out, 0)
        far_plane[f] = total.reshape(32, 128)

        def keep(at, s, message):
            far_line[f, s] = message

        assemble_at(far_plane.at[f], 0, 4, keep)
        copies = [send(far_plane.at[f], from_z.at[f, 0], z_send.at[f, 0], z_recv.at[f, 0], (far, n))]
        for s, (side, _) in enumerate(sides):
            copies.append(send(far_line.at[f, s], from_c.at[f, s, 0], c_send.at[f, s, 0], c_recv.at[f, s, 0], (far, side)))
        return total, copies

    def forward_face(f, far_part):
        radial_apply(zed, DERIV, -1, 0, 4)
        plane = slab(zed, 0)
        grad_a = along_mirrored(plane, DERIV, 1)
        grad_r = slab(radial_out, 0)
        add_slopes(0, plane)
        c = [planes[q].reshape(4, 8, 128) for q in range(6)]
        put(radial_in, 0, c[2] * plane + c[5] * grad_a + c[4] * grad_r)
        flux_a = c[1] * plane + c[3] * grad_a + c[5] * grad_r
        put(part_fz, 0, slab(metric.at[3], 0) * grad_a + slab(metric.at[4], 0) * grad_r)
        near_slope = slab(grad_z, 7)
        put(radial_in, 7, slab(part_fr, 7) + slab(metric.at[4], 7) * near_slope)
        radial_apply(radial_in, DERIV.T, -1, 0, 8)
        own = c[0] * plane + c[1] * grad_a + c[2] * grad_r + along_mirrored(flux_a, DERIV.T, -1) + slab(radial_out, 0)
        total = along_mirrored(slab(part_fa, 7) + slab(metric.at[3], 7) * near_slope, DERIV.T, -1)
        total = total + slab(metric.at[6], 7) * slab(zed, 7) + slab(radial_out, 7)
        for i in range(8):
            flux = slab(part_fz, i) + slab(metric.at[0], i) * slab(grad_z, i)
            put(part_fz, i, flux)
            total = total + flux * float(DERIV[i][7])
        put(fields.at[f], 0, own + far_part)
        put(fields.at[f], 7, total)
        return jnp.sum((far_part + own * 0.5) * plane + total * slab(zed, 7), axis=0)

    def forward_rest(f):
        energy = jnp.zeros((8, 128), F32)
        for i in INNER:
            slope = slab(grad_z, i)
            flux_a = slab(part_fa, i) + slab(metric.at[3], i) * slope
            put(radial_in, i, slab(part_fr, i) + slab(metric.at[4], i) * slope)
            put(part_fa, i, along_mirrored(flux_a, DERIV.T, -1) + slab(metric.at[6], i) * slab(zed, i))
        radial_apply(radial_in, DERIV.T, -1, 8, 24)
        for j in range(4):
            flux_z = [tile(part_fz, i, j) for i in range(8)]
            sums = [flux_z[m] + flux_z[7 - m] for m in range(4)]
            differences = [flux_z[m] - flux_z[7 - m] for m in range(4)]
            for i in range(1, 4):
                e, o = combine(even_t[i], sums), combine(odd_t[i], differences)
                for node_i, piece in ((i, e + o), (7 - i, o - e)):
                    total = piece + tile(part_fa, node_i, j) + tile(radial_out, node_i, j)
                    put_tile(fields.at[f], node_i, j, total)
                    energy = energy + total * tile(zed, node_i, j)
        return energy

    def assemble_own(f, start, count):
        def keep(at, s, message):
            faces[f, s, pl.ds(8 * at, 8), :] = message

        assemble_at(fields.at[f], start, count, keep)

    def assemble_at(ref, start, count, keep):
        low = pl.ds(8 * start, count, stride=8)
        high = pl.ds(8 * start + 7, count, stride=8)
        inner, outer = ref[low, :], ref[high, :]
        ref[low, :] = inner + jnp.where(radial_row > 0, pltpu.roll(outer, 1, 1), 0.0)
        ref[high, :] = outer + jnp.where(radial_row < 15, pltpu.roll(inner, 127, 1), 0.0)
        for at in range(start // 4, (start + count) // 4):
            row = ref[pl.ds(32 * at, 8), :]
            below = pltpu.roll(row, 16, 1)
            above = pltpu.roll(row, 112, 1)
            for s, (_, kind) in enumerate(sides):
                message = jnp.zeros_like(row)
                if kind in (0, 1):
                    message = jnp.where(lane < 16, below, message)
                if kind in (0, 2):
                    message = jnp.where(lane >= 112, above, message)
                keep(at, s, message)
            inside = jnp.where(lane < 64, pltpu.roll(row, 80, 1), pltpu.roll(row, 48, 1))
            ref[pl.ds(32 * at, 8), :] = row + jnp.where((lane >= 16) & (lane < 112), inside, 0.0)

    started = []

    def send(src, dst, send_sem, recv_sem, device):
        copy = pltpu.make_async_remote_copy(
            src_ref=src, dst_ref=dst, send_sem=send_sem, recv_sem=recv_sem, device_id=device, device_id_type=MESH
        )
        copy.start()
        started.append(copy)
        return copy

    def send_face(f, face, device):
        rows, line = pl.ds(32 * face, 32), pl.ds(8 * face, 8)
        copies = [
            send(fields.at[f, rows], from_z.at[f, face], z_send.at[f, face], z_recv.at[f, face], (device, n))
        ]
        for s, (side, _) in enumerate(sides):
            copies.append(
                send(faces.at[f, s, line], from_c.at[f, s, face], c_send.at[f, s, face], c_recv.at[f, s, face], (device, side))
            )
        return copies

    def send_cycle(f):
        return [
            send(faces.at[f, s], from_a.at[f, s], a_send.at[f, s], a_recv.at[f, s], (w, side))
            for s, (side, _) in enumerate(sides)
        ]

    def whole_plane(f, i):
        value = slab(fields.at[f], i)
        row = value[0]
        for s in range(len(sides)):
            row = row + from_a[f, s, pl.ds(8 * POS[i], 8), :]
        if i in FACE:
            come = from_z[f, POS[i]].reshape(4, 8, 128)
            row = row + come[0]
            for s in range(len(sides)):
                row = row + from_c[f, s, POS[i]]
            return jnp.concatenate([row[None], value[1:] + come[1:]], axis=0)
        return jnp.concatenate([row[None], value[1:]], axis=0)

    def wait_all(copies):
        for copy in copies:
            copy.wait_recv()

    def weighted(one, two, chosen=range(8)):
        total = None
        for i in chosen:
            product = one(i) * two(i)
            term = (product[1] + product[2]) + product[3] + product[0] * 0.5
            if i in (0, 7):
                term = term * 0.5
            total = term if total is None else total + term
        shared = ((node == 0) & (radial > 0)) | ((node == 7) & (radial < 15))
        return jnp.where(shared, total * 0.5, total)

    def stack_rows(terms):
        out = jnp.zeros((8, 128), F32)
        for q, term in enumerate(terms):
            out = jnp.where(node == q, jnp.sum(term, axis=0, keepdims=True), out)
        return out

    counts = [len(partners) for partners in phases]

    def sum_start(r, p, value):
        part[r, p] = value
        at = sum(counts[:p])
        return [
            send(part.at[r, p], gathered.at[r, at + q], g_send.at[r, at + q], g_recv.at[r, at + q], device)
            for q, device in enumerate(phases[p])
        ]

    def sum_end(r, p, copies):
        at = sum(counts[:p])
        total = part[r, p]
        for q, copy in enumerate(copies):
            copy.wait_recv()
            total = total + gathered[r, at + q]
        return total

    def sum_rest(r, p, copies):
        total = sum_end(r, p, copies)
        for later in range(p + 1, len(phases)):
            total = sum_end(r, later, sum_start(r, later, total))
        return jnp.sum(total, axis=1, keepdims=True)

    center = (interval_high + interval_low) / 2.0
    half_width = (interval_high - interval_low) / 2.0
    sigma = center / half_width
    rhos = [1.0 / sigma]
    for _ in range(2):
        rhos.append(1.0 / (2.0 * sigma - rhos[-1]))

    assemble_own(0, 0, 32)
    for i in range(8):
        bound_fluxes(i)
    part_z = along_eight(h_z, ABS.T, 1)
    radial_apply(radial_in, ABS.T, 1, 0, 8)
    for i in FACE:
        bound_total(i, part_z)
    assemble_own(1, 0, 8)
    pl.semaphore_wait(barrier, len(greeted))
    from_far = send_face(1, 0, far) + send_face(0, 0, far)
    from_near = send_face(1, 1, near) + send_face(0, 1, near)
    corner = float(DERIV[0][0])
    own = slab(metric.at[6], 0)
    for i in range(8):
        own = own + slab(metric.at[0], i) * float(DERIV[i][0] ** 2)
    for q, plane in enumerate(
        (
            own,
            slab(metric.at[3], 0) * (mirror * pipe_mirror * corner),
            slab(metric.at[4], 0) * (pipe_mirror * corner),
            slab(metric.at[1], 0),
            slab(metric.at[2], 0),
            slab(metric.at[5], 0) * mirror,
        )
    ):
        planes[q] = plane.reshape(32, 128)
    planes_copy = pltpu.make_async_remote_copy(
        src_ref=planes,
        dst_ref=from_planes,
        send_sem=p_send.at[0],
        recv_sem=p_recv.at[0],
        device_id=(far, n),
        device_id_type=MESH,
    )
    planes_copy.start()
    radial_apply(radial_in, ABS.T, 1, 8, 24)
    for i in INNER:
        bound_total(i, part_z)
    assemble_own(1, 8, 24)
    cycle = send_cycle(1) + send_cycle(0)
    metric[3] = metric[3] * (mirror * pipe_mirror)
    metric[4] = metric[4] * pipe_mirror
    metric[5] = metric[5] * mirror

    def begin(i):
        inverse = 1.0 / whole_plane(1, i)
        load_plane = whole_plane(0, i)
        update = load_plane * inverse * (1.0 / center)
        put(binv, i, inverse)
        put(res, i, load_plane)
        put(zed, i, update)
        put(dee, i, update)

    wait_all(cycle)
    for i in INNER:
        begin(i)
    forward_inner()
    wait_all(from_near)
    begin(7)
    pending = [from_far, lambda: begin(0)]

    def both_faces(f, meanwhile=None):
        far_part, copies = forward_far(f)
        if meanwhile is not None:
            meanwhile()
        wait_all(pending[0])
        pending[1]()
        if f == 2:
            planes_copy.wait()
            planes[...] = planes[...] + from_planes[...]
        energy = forward_face(f, far_part)
        assemble_own(f, 0, 8)
        return energy, copies, send_face(f, 1, near)

    def apply_then(f, update, between=None, meanwhile=None):
        energy, from_far, from_near = both_faces(f, meanwhile)
        energy = energy + forward_rest(f)
        assemble_own(f, 8, 24)
        cycle = send_cycle(f)
        after = between(energy) if between is not None else None
        wait_all(cycle)
        for i in INNER:
            update(i, whole_plane(f, i))
        forward_inner()
        wait_all(from_near)
        update(7, whole_plane(f, 7))
        pending[:] = [from_far, lambda: update(0, whole_plane(f, 0))]
        return after

    def smoothed(source, step, i, plane):
        now, later = rhos[step], rhos[step + 1]
        return slab(dee, i) * (now * later) + slab(binv, i) * (slab(source, i) - plane) * (2.0 * later / half_width)

    def smooth(source, step):
        def update(i, plane):
            change = smoothed(source, step, i, plane)
            put(dee, i, change)
            put(zed, i, slab(zed, i) + change)

        return update

    apply_then(2, smooth(res, 0))
    apply_then(3, smooth(res, 1))

    def start_norm(energy):
        norm = weighted(lambda i: slab(res, i), lambda i: slab(zed, i))
        return sum_start(0, 0, stack_rows([norm, energy]))

    def restart(i, plane):
        put(image, i, plane)
        put(first, i, slab(zed, i))
        update = plane * slab(binv, i) * (1.0 / center)
        put(zed, i, update)
        put(dee, i, update)

    sums = apply_then(4, restart, start_norm)
    more = apply_then(5, smooth(image, 0), lambda energy: sum_start(0, 1, sum_end(0, 0, sums)))
    scalars = {}

    def finish_norm(energy):
        total = sum_rest(0, 1, more)
        scalars["norm"], scalars["energy"] = total[0:1], total[1:2]
        scalars["alpha"] = total[0:1] / total[1:2]

    def step_on(i, plane):
        end = slab(zed, i) + smoothed(image, 1, i, plane)
        put(res, i, slab(res, i) - scalars["alpha"] * slab(image, i))
        put(zed, i, slab(first, i) - scalars["alpha"] * end)

    def read_back(value_of, chosen):
        rows = []
        for i in chosen:
            value = jnp.where(odd_row, value_of(7 - i), value_of(i))
            for j in range(8):
                keep = (lane < 64) if j < 4 else (lane >= 64)
                rows.append(jnp.where(keep, value[j if j < 4 else 7 - j], 0.0))
        full = jnp.stack(rows).reshape(64 * len(chosen), 128)
        high = full.astype(jnp.bfloat16)
        low = (full - high.astype(F32)).astype(jnp.bfloat16)
        dims = (((1,), (1,)), ((), ()))
        return lax.dot_general(hot_both, high, dims, preferred_element_type=F32) + lax.dot_general(
            hot_both, low, dims, preferred_element_type=F32
        )

    def read_first():
        read[0] = read_back(lambda i: slab(first, i), range(8))

    apply_then(6, step_on, finish_norm, read_first)
    norm_0, energy_0, alpha_0 = scalars["norm"], scalars["energy"], scalars["alpha"]

    sums_of = {}

    def norm_and_cross(chosen):
        return (
            weighted(lambda i: slab(res, i), lambda i: slab(zed, i), chosen),
            weighted(lambda i: slab(zed, i), lambda i: slab(image, i), chosen),
        )

    def prepare():
        sums_of["norm"], sums_of["cross"] = norm_and_cross(range(1, 8))
        read[3] = read_back(lambda i: slab(image, i), range(8))

    energy, from_far, from_near = both_faces(7, prepare)
    norm, cross = norm_and_cross([0])
    norm, cross = norm + sums_of["norm"], cross + sums_of["cross"]
    energy = energy + forward_rest(7)
    sums = sum_start(1, 0, stack_rows([norm, cross, energy]))
    assemble_own(7, 8, 24)
    cycle = send_cycle(7)
    read[1] = read_back(lambda i: slab(zed, i), range(8))
    totals = sum_end(1, 0, sums)
    for later in range(1, len(phases) - 1):
        totals = sum_end(1, later, sum_start(1, later, totals))
    sums = sum_start(1, len(phases) - 1, totals)
    read[2] = read_back(lambda i: slab(res, i), range(8))
    wait_all(cycle)
    middle = read_back(lambda i: whole_plane(7, i), range(2, 6))
    total = jnp.sum(sum_end(1, len(phases) - 1, sums), axis=1, keepdims=True)
    norm_1, cross_1, energy_1 = total[0:1], total[1:2], total[2:3]
    beta = norm_1 / norm_0
    alpha_1 = norm_1 / (energy_1 + 2.0 * beta * cross_1 + beta * beta * energy_0)
    solution_ref[...] = (alpha_0 + alpha_1 * beta) * read[0] + alpha_1 * read[1]
    residual = read[2] - (alpha_1 * beta) * read[3]
    residual_ref[:, 128:384] = residual[:, 128:384] - alpha_1 * middle
    wait_all(from_near)
    wait_all(from_far)
    ends = read_back(lambda i: whole_plane(7, i), (0, 1, 6, 7))
    residual_ref[:, 0:128] = residual[:, 0:128] - alpha_1 * ends[:, 0:128]
    residual_ref[:, 384:512] = residual[:, 384:512] - alpha_1 * ends[:, 128:256]
    for copy in started:
        copy.wait_send()


def solution(mesh):
    n_wide, n_narrow = mesh.shape["wide"], mesh.shape["narrow"]
    sides = 1 if n_narrow == 2 else 2
    factors = wide_factors(n_wide)
    partners = n_narrow * factors[0] - 1 + sum(factor - 1 for factor in factors[1:])
    vmem = pltpu.VMEM
    block = vmem((256, 128), F32)
    dma = pltpu.SemaphoreType.DMA

    def local(load, geom, element_order):
        whole = pl.BlockSpec(memory_space=pltpu.VMEM)
        shape = jax.ShapeDtypeStruct(load.shape, F32)
        return pl.pallas_call(
            functools.partial(body, n_wide, n_narrow),
            out_shape=(shape, shape),
            in_specs=[pl.BlockSpec(memory_space=pltpu.HBM)] * 3,
            out_specs=(whole, whole),
            scratch_shapes=[
                vmem(load.shape, F32),
                vmem(geom.shape, geom.dtype),
                vmem(element_order.shape, jnp.int32),
                vmem((7, 256, 128), F32),
                block,
                block,
                block,
                block,
                block,
                block,
                vmem((FIELDS, 256, 128), F32),
                vmem((FIELDS, sides, 64, 128), F32),
                vmem((FIELDS, 32, 128), F32),
                vmem((FIELDS, sides, 8, 128), F32),
                vmem((6, 32, 128), F32),
                vmem((6, 32, 128), F32),
                block,
                block,
                block,
                block,
                block,
                block,
                vmem((4, 64, 512), F32),
                vmem((2, len(factors), 8, 128), F32),
                vmem((FIELDS, 2, 32, 128), F32),
                vmem((FIELDS, sides, 64, 128), F32),
                vmem((FIELDS, sides, 2, 8, 128), F32),
                vmem((2, partners, 8, 128), F32),
                dma((FIELDS, 2)),
                dma((FIELDS, 2)),
                dma((FIELDS, sides)),
                dma((FIELDS, sides)),
                dma((FIELDS, sides, 2)),
                dma((FIELDS, sides, 2)),
                dma((2, partners)),
                dma((2, partners)),
                dma((3,)),
                dma((1,)),
                dma((1,)),
            ],
            compiler_params=pltpu.CompilerParams(
                collective_id=0, has_side_effects=True, vmem_limit_bytes=60 * 1024 * 1024
            ),
        )(load, geom, element_order)

    return jax.shard_map(
        local,
        mesh=mesh,
        in_specs=(
            P(("wide", "narrow"), None),
            P(None, ("wide", "narrow"), None),
            P("wide", "narrow", None),
        ),
        out_specs=(P(("wide", "narrow"), None), P(("wide", "narrow"), None)),
        check_vma=False,
    )
```

```python
import functools

import jax
import jax.numpy as jnp
import numpy as np
from jax import lax
from jax.experimental import pallas as pl
from jax.experimental.pallas import tpu as pltpu
from jax.sharding import PartitionSpec as P

MESH = pl.DeviceIdType.MESH
interval_low = 0.03
interval_high = 1.0
FIELDS = 8
F32 = jnp.float32


ORDER = [0, 7, 1, 6, 2, 5, 3, 4]
POS = [ORDER.index(i) for i in range(8)]
FACE = [0, 7]
INNER = [1, 6, 2, 5, 3, 4]


def legendre_seven(point):
    before = 1.0
    current = point
    for degree in range(1, 7):
        after = ((2.0 * degree + 1.0) * point * current - degree * before) / (degree + 1.0)
        before = current
        current = after
    return current


def gll_derivative():
    points = 8
    inner_nodes = [
        -0.8717401485096066,
        -0.5917001814331423,
        -0.2092992179024789,
        0.2092992179024789,
        0.5917001814331423,
        0.8717401485096066,
    ]
    nodes = [-1.0] + inner_nodes + [1.0]
    values_at = [legendre_seven(node) for node in nodes]
    matrix = np.zeros((points, points))
    for source in range(points):
        for target in range(points):
            if source != target:
                matrix[source, target] = values_at[source] / (
                    values_at[target] * (nodes[source] - nodes[target])
                )
    matrix[0, 0] = -(points - 1) * points / 4.0
    matrix[points - 1, points - 1] = (points - 1) * points / 4.0
    return matrix


DERIV = gll_derivative()
ABS = np.abs(DERIV)
ROW_TOTAL = ABS.sum(axis=1)


def halves(matrix):
    even = (matrix[:4, :4] + matrix[:4, :3:-1]) / 2.0
    odd = (matrix[:4, :4] - matrix[:4, :3:-1]) / 2.0
    return even, odd


def combine(row, terms):
    total = terms[0] * float(row[0])
    for factor, term in zip(row[1:], terms[1:]):
        total = total + term * float(factor)
    return total


def along_eight(values, matrix, parity):
    even, odd = halves(matrix)
    sums = [values[m] + values[7 - m] for m in range(4)]
    differences = [values[m] - values[7 - m] for m in range(4)]
    result = [None] * 8
    for i in range(4):
        e = combine(even[i], sums)
        o = combine(odd[i], differences)
        result[i] = e + o
        result[7 - i] = (e - o) if parity > 0 else (o - e)
    return result


def lane_roll(value, shift):
    shape = value.shape
    flat = value.reshape(-1, shape[-1])
    return pltpu.roll(flat, shift, 1).reshape(shape)


def along_mirrored(value, matrix, sign):
    even, odd = halves(matrix)
    other = lane_roll(value, 64)
    plus, minus = value + other, value - other
    sums, differences = (plus, minus) if sign > 0 else (minus, plus)
    rows = []
    for j in range(4):
        rows.append(
            combine(even[j], [sums[m] for m in range(4)])
            + combine(odd[j], [differences[m] for m in range(4)])
        )
    return jnp.stack(rows)


def wide_factors(count):
    factors = []
    while count > 1:
        for factor in (4, 3, 2, 5, 7):
            if count % factor == 0:
                break
        else:
            factor = count
        factors.append(factor)
        count //= factor
    return factors


def body(
    n_wide,
    n_narrow,
    load_hbm,
    geom_hbm,
    order_hbm,
    solution_ref,
    residual_ref,
    load_ref,
    geom_ref,
    order_ref,
    metric,
    radial_in,
    radial_out,
    part_fz,
    part_fa,
    part_fr,
    grad_z,
    fields,
    faces,
    far_plane,
    far_line,
    planes,
    from_planes,
    res,
    binv,
    zed,
    dee,
    image,
    first,
    read,
    part,
    from_z,
    from_a,
    from_c,
    gathered,
    z_send,
    z_recv,
    a_send,
    a_recv,
    c_send,
    c_recv,
    g_send,
    g_recv,
    in_sem,
    p_send,
    p_recv,
):
    fetches = [
        pltpu.make_async_copy(order_hbm, order_ref, in_sem.at[0]),
        pltpu.make_async_copy(load_hbm, load_ref, in_sem.at[1]),
        pltpu.make_async_copy(geom_hbm, geom_ref, in_sem.at[2]),
    ]
    for fetch in fetches:
        fetch.start()
    w = lax.axis_index("wide")
    n = lax.axis_index("narrow")
    odd_one = lax.rem(w, 2)
    near = lax.rem(w + n_wide + 1 - 2 * odd_one, n_wide)
    far = lax.rem(w + n_wide - 1 + 2 * odd_one, n_wide)
    if n_narrow == 2:
        sides = [(lax.rem(n + 1, 2), 0)]
    else:
        sides = [(lax.rem(n + 1, n_narrow), 1), (lax.rem(n + n_narrow - 1, n_narrow), 2)]

    phases = []
    stride = 1
    for number, factor in enumerate(wide_factors(n_wide)):
        place = lax.rem(w // stride, factor)
        base = w - place * stride
        partners = []
        for dn in range(n_narrow if number == 0 else 1):
            for dw in range(factor):
                if dn == 0 and dw == 0:
                    continue
                there = base + lax.rem(place + dw, factor) * stride
                partners.append((there, lax.rem(n + dn, n_narrow)))
        phases.append(partners)
        stride *= factor

    barrier = pltpu.get_barrier_semaphore()
    greeted = [(near, n), (far, n)]
    for side, _ in sides:
        greeted += [(near, side), (far, side), (w, side)]
    for partners in phases:
        greeted += partners
    for device in greeted:
        pl.semaphore_signal(barrier, inc=1, device_id=device, device_id_type=MESH)

    lane = lax.broadcasted_iota(jnp.int32, (8, 128), 1)
    node = lax.broadcasted_iota(jnp.int32, (8, 128), 0)
    radial = lane % 16
    lane_row = lax.broadcasted_iota(jnp.int32, (1, 128), 1)
    mirror = jnp.where(lane_row < 64, 1.0, -1.0).astype(F32)
    radial_row = lane_row % 16
    odd_row = (lane_row * 0 + odd_one) == 1
    pipe_mirror = jnp.where(odd_row, -1.0, 1.0).astype(F32)

    fetches[0].wait()
    fetches[1].wait()
    order = order_ref[0].astype(jnp.int32)
    order_twice = jnp.concatenate([order, order + 64], axis=1)
    hot_t = (lax.broadcasted_iota(jnp.int32, (128, 128), 0) == order_twice).astype(F32)
    hot = jnp.transpose(hot_t)
    hot_both = (hot[:64] + hot[64:]).astype(jnp.bfloat16)
    top, bottom = hot[:64], hot[64:]
    zero = jnp.zeros_like(top)
    into_low = jnp.concatenate(
        [jnp.concatenate([top, zero], axis=1), jnp.concatenate([zero, top], axis=1)], axis=0
    ).astype(jnp.bfloat16)
    into_high = jnp.concatenate(
        [jnp.concatenate([bottom, zero], axis=1), jnp.concatenate([zero, bottom], axis=1)], axis=0
    ).astype(jnp.bfloat16)

    def oriented(value):
        pairs = value.reshape(4, 2, 32, 128)
        swapped = jnp.stack([pairs[:, 1], pairs[:, 0]], axis=1).reshape(256, 128)
        return jnp.where(odd_row, swapped, value)

    def place_pair(one, two):
        turned = jnp.transpose(jnp.concatenate([one, two], axis=0)).astype(F32)
        split = turned.reshape(8, 8, 8, 128)
        low = jnp.stack([split[i, j] for i in ORDER for j in range(4)]).reshape(256, 128).astype(jnp.bfloat16)
        high = jnp.stack([split[i, 7 - j] for i in ORDER for j in range(4)]).reshape(256, 128).astype(jnp.bfloat16)
        both = jnp.dot(low, into_low, preferred_element_type=F32)
        both = both + jnp.dot(high, into_high, preferred_element_type=F32)
        one, two = both[:, :128], both[:, 128:]
        return oriented(one), oriented(two)

    def rounded(value):
        return value.astype(jnp.bfloat16)

    load = load_ref[...]
    load_high = rounded(load)
    load_rest = load - load_high.astype(F32)
    load_mid = rounded(load_rest)
    load_low = rounded(load_rest - load_mid.astype(F32))
    fetches[2].wait()
    g = [geom_ref[q] for q in range(7)]
    for q in (0, 2, 4):
        metric[q], metric[q + 1] = place_pair(g[q], g[q + 1])
    metric[6], grid_high = place_pair(g[6], load_high)
    grid_mid, grid_low = place_pair(load_mid, load_low)
    fields[0] = grid_high + (grid_mid + grid_low)

    def slab(ref, i):
        return ref[pl.ds(32 * POS[i], 32), :].reshape(4, 8, 128)

    def put(ref, i, value):
        ref[pl.ds(32 * POS[i], 32), :] = value.reshape(32, 128)

    def radial_apply(source, matrix, parity, start=0, count=32):
        values = [source[pl.ds(8 * start + k, count, stride=8), :] for k in range(8)]
        result = along_eight(values, matrix, parity)
        for k in range(8):
            radial_out[pl.ds(8 * start + k, count, stride=8), :] = result[k]

    q_r = jnp.full((8, 128), float(ROW_TOTAL[0]), F32)
    for k in range(1, 4):
        q_r = jnp.where((node == k) | (node == 7 - k), float(ROW_TOTAL[k]), q_r)
    h_z, part_a = [None] * 8, [None] * 8

    def by_cycle(value):
        return jnp.stack([value[j] * float(ROW_TOTAL[j]) for j in range(4)])

    def bound_fluxes(i):
        a = [jnp.abs(slab(metric.at[q], i)) for q in range(6)]
        q_z = float(ROW_TOTAL[i])
        h_z[i] = a[0] * q_z + by_cycle(a[3]) + a[4] * q_r
        part_a[i] = along_mirrored(a[3] * q_z + by_cycle(a[1]) + a[5] * q_r, ABS.T, 1)
        put(radial_in, i, a[4] * q_z + by_cycle(a[5]) + a[2] * q_r)

    def bound_total(i, part_z):
        put(fields.at[1], i, part_z[i] + part_a[i] + slab(radial_out, i) + jnp.abs(slab(metric.at[6], i)))

    even, odd = halves(DERIV)
    even_t, odd_t = halves(DERIV.T)

    def forward_inner():
        radial_apply(zed, DERIV, -1, 8, 24)
        for i in INNER:
            grad_a = along_mirrored(slab(zed, i), DERIV, 1)
            grad_r = slab(radial_out, i)
            put(part_fz, i, slab(metric.at[3], i) * grad_a + slab(metric.at[4], i) * grad_r)
            put(part_fa, i, slab(metric.at[1], i) * grad_a + slab(metric.at[5], i) * grad_r)
            put(part_fr, i, slab(metric.at[5], i) * grad_a + slab(metric.at[2], i) * grad_r)
        for j in range(4):
            v = [tile(zed, i, j) for i in range(1, 7)]
            sums = [v[m] + v[5 - m] for m in range(3)]
            differences = [v[m] - v[5 - m] for m in range(3)]
            for i in range(4):
                e, o = combine(even[i][1:], sums), combine(odd[i][1:], differences)
                put_tile(grad_z, i, j, e + o)
                put_tile(grad_z, 7 - i, j, o - e)

    def tile(ref, i, j):
        return ref[pl.ds(32 * POS[i] + 8 * j, 8), :]

    def put_tile(ref, i, j, value):
        ref[pl.ds(32 * POS[i] + 8 * j, 8), :] = value

    def add_slopes(column, plane):
        for i in range(8):
            put(grad_z, i, slab(grad_z, i) + plane * float(DERIV[i][column]))

    def forward_far(f):
        radial_apply(zed, DERIV, -1, 4, 4)
        plane = slab(zed, 7)
        grad_a = along_mirrored(plane, DERIV, 1)
        grad_r = slab(radial_out, 7)
        add_slopes(7, plane)
        put(part_fz, 7, slab(metric.at[3], 7) * grad_a + slab(metric.at[4], 7) * grad_r)
        put(part_fa, 7, slab(metric.at[1], 7) * grad_a + slab(metric.at[5], 7) * grad_r)
        put(part_fr, 7, slab(metric.at[5], 7) * grad_a + slab(metric.at[2], 7) * grad_r)
        slope = slab(grad_z, 0)
        put(radial_in, 0, slab(metric.at[4], 0) * slope)
        radial_apply(radial_in, DERIV.T, -1, 0, 4)
        total = along_mirrored(slab(metric.at[3], 0) * slope, DERIV.T, -1) + slab(metric.at[0], 0) * slope * float(DERIV[0][0])
        for i in range(1, 8):
            flux = slab(part_fz, i) + slab(metric.at[0], i) * slab(grad_z, i)
            total = total + flux * float(DERIV[i][0])
        total = total + slab(radial_out, 0)
        far_plane[f] = total.reshape(32, 128)

        def keep(at, s, message):
            far_line[f, s] = message

        assemble_at(far_plane.at[f], 0, 4, keep)
        copies = [send(far_plane.at[f], from_z.at[f, 0], z_send.at[f, 0], z_recv.at[f, 0], (far, n))]
        for s, (side, _) in enumerate(sides):
            copies.append(send(far_line.at[f, s], from_c.at[f, s, 0], c_send.at[f, s, 0], c_recv.at[f, s, 0], (far, side)))
        return total, copies

    def forward_face(f, far_part):
        radial_apply(zed, DERIV, -1, 0, 4)
        plane = slab(zed, 0)
        grad_a = along_mirrored(plane, DERIV, 1)
        grad_r = slab(radial_out, 0)
        add_slopes(0, plane)
        c = [planes[q].reshape(4, 8, 128) for q in range(6)]
        put(radial_in, 0, c[2] * plane + c[5] * grad_a + c[4] * grad_r)
        flux_a = c[1] * plane + c[3] * grad_a + c[5] * grad_r
        put(part_fz, 0, slab(metric.at[3], 0) * grad_a + slab(metric.at[4], 0) * grad_r)
        near_slope = slab(grad_z, 7)
        put(radial_in, 7, slab(part_fr, 7) + slab(metric.at[4], 7) * near_slope)
        radial_apply(radial_in, DERIV.T, -1, 0, 8)
        own = c[0] * plane + c[1] * grad_a + c[2] * grad_r + along_mirrored(flux_a, DERIV.T, -1) + slab(radial_out, 0)
        total = along_mirrored(slab(part_fa, 7) + slab(metric.at[3], 7) * near_slope, DERIV.T, -1)
        total = total + slab(metric.at[6], 7) * slab(zed, 7) + slab(radial_out, 7)
        for i in range(8):
            flux = slab(part_fz, i) + slab(metric.at[0], i) * slab(grad_z, i)
            put(part_fz, i, flux)
            total = total + flux * float(DERIV[i][7])
        put(fields.at[f], 0, own + far_part)
        put(fields.at[f], 7, total)
        return jnp.sum((far_part + own * 0.5) * plane + total * slab(zed, 7), axis=0)

    def forward_rest(f):
        energy = jnp.zeros((8, 128), F32)
        for i in INNER:
            slope = slab(grad_z, i)
            flux_a = slab(part_fa, i) + slab(metric.at[3], i) * slope
            put(radial_in, i, slab(part_fr, i) + slab(metric.at[4], i) * slope)
            put(part_fa, i, along_mirrored(flux_a, DERIV.T, -1) + slab(metric.at[6], i) * slab(zed, i))
        radial_apply(radial_in, DERIV.T, -1, 8, 24)
        copies = None
        for j in range(4):
            if j == 1:
                copies = send_edges(f)
            flux_z = [tile(part_fz, i, j) for i in range(8)]
            sums = [flux_z[m] + flux_z[7 - m] for m in range(4)]
            differences = [flux_z[m] - flux_z[7 - m] for m in range(4)]
            for i in range(1, 4):
                e, o = combine(even_t[i], sums), combine(odd_t[i], differences)
                for node_i, piece in ((i, e + o), (7 - i, o - e)):
                    total = piece + tile(part_fa, node_i, j) + tile(radial_out, node_i, j)
                    put_tile(fields.at[f], node_i, j, total)
                    energy = energy + total * tile(zed, node_i, j)
        return energy, copies

    def send_edges(f):
        for i in INNER:
            row = tile(fields.at[f], i, 0)
            down_one = pltpu.roll(pltpu.roll(row, 1, 0), 1, 1)
            up_one = pltpu.roll(pltpu.roll(row, 7, 0), 127, 1)
            row = row + jnp.where((node == 0) & (radial > 0), down_one, 0.0)
            row = row + jnp.where((node == 7) & (radial < 15), up_one, 0.0)
            keep_line(f, POS[i], row)
        return send_cycle(f)

    def keep_line(f, at, row):
        below = pltpu.roll(row, 16, 1)
        above = pltpu.roll(row, 112, 1)
        for s, (_, kind) in enumerate(sides):
            message = jnp.zeros_like(row)
            if kind in (0, 1):
                message = jnp.where(lane < 16, below, message)
            if kind in (0, 2):
                message = jnp.where(lane >= 112, above, message)
            faces[f, s, pl.ds(8 * at, 8), :] = message

    def assemble_own(f, start, count):
        def keep(at, s, message):
            if f < 2 or at < 2:
                faces[f, s, pl.ds(8 * at, 8), :] = message

        assemble_at(fields.at[f], start, count, keep)

    def assemble_at(ref, start, count, keep):
        low = pl.ds(8 * start, count, stride=8)
        high = pl.ds(8 * start + 7, count, stride=8)
        inner, outer = ref[low, :], ref[high, :]
        ref[low, :] = inner + jnp.where(radial_row > 0, pltpu.roll(outer, 1, 1), 0.0)
        ref[high, :] = outer + jnp.where(radial_row < 15, pltpu.roll(inner, 127, 1), 0.0)
        for at in range(start // 4, (start + count) // 4):
            row = ref[pl.ds(32 * at, 8), :]
            below = pltpu.roll(row, 16, 1)
            above = pltpu.roll(row, 112, 1)
            for s, (_, kind) in enumerate(sides):
                message = jnp.zeros_like(row)
                if kind in (0, 1):
                    message = jnp.where(lane < 16, below, message)
                if kind in (0, 2):
                    message = jnp.where(lane >= 112, above, message)
                keep(at, s, message)
            inside = jnp.where(lane < 64, pltpu.roll(row, 80, 1), pltpu.roll(row, 48, 1))
            ref[pl.ds(32 * at, 8), :] = row + jnp.where((lane >= 16) & (lane < 112), inside, 0.0)

    started = []

    def send(src, dst, send_sem, recv_sem, device):
        copy = pltpu.make_async_remote_copy(
            src_ref=src, dst_ref=dst, send_sem=send_sem, recv_sem=recv_sem, device_id=device, device_id_type=MESH
        )
        copy.start()
        started.append(copy)
        return copy

    def send_face(f, face, device):
        rows, line = pl.ds(32 * face, 32), pl.ds(8 * face, 8)
        copies = [
            send(fields.at[f, rows], from_z.at[f, face], z_send.at[f, face], z_recv.at[f, face], (device, n))
        ]
        for s, (side, _) in enumerate(sides):
            copies.append(
                send(faces.at[f, s, line], from_c.at[f, s, face], c_send.at[f, s, face], c_recv.at[f, s, face], (device, side))
            )
        return copies

    def send_cycle(f):
        return [
            send(faces.at[f, s], from_a.at[f, s], a_send.at[f, s], a_recv.at[f, s], (w, side))
            for s, (side, _) in enumerate(sides)
        ]

    def whole_plane(f, i):
        value = slab(fields.at[f], i)
        row = value[0]
        for s in range(len(sides)):
            row = row + from_a[f, s, pl.ds(8 * POS[i], 8), :]
        if i in FACE:
            come = from_z[f, POS[i]].reshape(4, 8, 128)
            row = row + come[0]
            for s in range(len(sides)):
                row = row + from_c[f, s, POS[i]]
            return jnp.concatenate([row[None], value[1:] + come[1:]], axis=0)
        return jnp.concatenate([row[None], value[1:]], axis=0)

    def wait_all(copies):
        for copy in copies:
            copy.wait_recv()

    def weighted(one, two, chosen=range(8)):
        total = None
        for i in chosen:
            product = one(i) * two(i)
            term = (product[1] + product[2]) + product[3] + product[0] * 0.5
            if i in (0, 7):
                term = term * 0.5
            total = term if total is None else total + term
        shared = ((node == 0) & (radial > 0)) | ((node == 7) & (radial < 15))
        return jnp.where(shared, total * 0.5, total)

    def stack_rows(terms):
        out = jnp.zeros((8, 128), F32)
        for q, term in enumerate(terms):
            out = jnp.where(node == q, jnp.sum(term, axis=0, keepdims=True), out)
        return out

    counts = [len(partners) for partners in phases]

    def sum_start(r, p, value):
        part[r, p] = value
        at = sum(counts[:p])
        return [
            send(part.at[r, p], gathered.at[r, at + q], g_send.at[r, at + q], g_recv.at[r, at + q], device)
            for q, device in enumerate(phases[p])
        ]

    def sum_end(r, p, copies):
        at = sum(counts[:p])
        total = part[r, p]
        for q, copy in enumerate(copies):
            copy.wait_recv()
            total = total + gathered[r, at + q]
        return total

    def sum_rest(r, p, copies):
        total = sum_end(r, p, copies)
        for later in range(p + 1, len(phases)):
            total = sum_end(r, later, sum_start(r, later, total))
        return jnp.sum(total, axis=1, keepdims=True)

    center = (interval_high + interval_low) / 2.0
    half_width = (interval_high - interval_low) / 2.0
    sigma = center / half_width
    rhos = [1.0 / sigma]
    for _ in range(2):
        rhos.append(1.0 / (2.0 * sigma - rhos[-1]))

    assemble_own(0, 0, 32)
    for i in range(8):
        bound_fluxes(i)
    part_z = along_eight(h_z, ABS.T, 1)
    radial_apply(radial_in, ABS.T, 1, 0, 8)
    for i in FACE:
        bound_total(i, part_z)
    assemble_own(1, 0, 8)
    pl.semaphore_wait(barrier, len(greeted))
    from_far = send_face(1, 0, far) + send_face(0, 0, far)
    from_near = send_face(1, 1, near) + send_face(0, 1, near)
    corner = float(DERIV[0][0])
    own = slab(metric.at[6], 0)
    for i in range(8):
        own = own + slab(metric.at[0], i) * float(DERIV[i][0] ** 2)
    for q, plane in enumerate(
        (
            own,
            slab(metric.at[3], 0) * (mirror * pipe_mirror * corner),
            slab(metric.at[4], 0) * (pipe_mirror * corner),
            slab(metric.at[1], 0),
            slab(metric.at[2], 0),
            slab(metric.at[5], 0) * mirror,
        )
    ):
        planes[q] = plane.reshape(32, 128)
    planes_copy = pltpu.make_async_remote_copy(
        src_ref=planes,
        dst_ref=from_planes,
        send_sem=p_send.at[0],
        recv_sem=p_recv.at[0],
        device_id=(far, n),
        device_id_type=MESH,
    )
    planes_copy.start()
    radial_apply(radial_in, ABS.T, 1, 8, 24)
    for i in INNER:
        bound_total(i, part_z)
    assemble_own(1, 8, 24)
    cycle = send_cycle(1) + send_cycle(0)
    metric[3] = metric[3] * (mirror * pipe_mirror)
    metric[4] = metric[4] * pipe_mirror
    metric[5] = metric[5] * mirror

    def begin(i):
        inverse = 1.0 / whole_plane(1, i)
        load_plane = whole_plane(0, i)
        update = load_plane * inverse * (1.0 / center)
        put(binv, i, inverse)
        put(res, i, load_plane)
        put(zed, i, update)
        put(dee, i, update)

    wait_all(cycle)
    for i in INNER:
        begin(i)
    forward_inner()
    wait_all(from_near)
    begin(7)
    pending = [from_far, lambda: begin(0)]

    def both_faces(f, meanwhile=None):
        far_part, copies = forward_far(f)
        if meanwhile is not None:
            meanwhile()
        wait_all(pending[0])
        pending[1]()
        if f == 2:
            planes_copy.wait()
            planes[...] = planes[...] + from_planes[...]
        energy = forward_face(f, far_part)
        assemble_own(f, 0, 8)
        return energy, copies, send_face(f, 1, near)

    def apply_then(f, update, between=None, meanwhile=None):
        energy, from_far, from_near = both_faces(f, meanwhile)
        more, cycle = forward_rest(f)
        energy = energy + more
        assemble_own(f, 8, 24)
        after = between(energy) if between is not None else None
        wait_all(cycle)
        for i in INNER:
            update(i, whole_plane(f, i))
        forward_inner()
        wait_all(from_near)
        update(7, whole_plane(f, 7))
        pending[:] = [from_far, lambda: update(0, whole_plane(f, 0))]
        return after

    def smoothed(source, step, i, plane):
        now, later = rhos[step], rhos[step + 1]
        return slab(dee, i) * (now * later) + slab(binv, i) * (slab(source, i) - plane) * (2.0 * later / half_width)

    def smooth(source, step):
        def update(i, plane):
            change = smoothed(source, step, i, plane)
            put(dee, i, change)
            put(zed, i, slab(zed, i) + change)

        return update

    apply_then(2, smooth(res, 0))
    apply_then(3, smooth(res, 1))

    def start_norm(energy):
        norm = weighted(lambda i: slab(res, i), lambda i: slab(zed, i))
        return sum_start(0, 0, stack_rows([norm, energy]))

    def restart(i, plane):
        put(image, i, plane)
        put(first, i, slab(zed, i))
        update = plane * slab(binv, i) * (1.0 / center)
        put(zed, i, update)
        put(dee, i, update)

    sums = apply_then(4, restart, start_norm)
    more = apply_then(5, smooth(image, 0), lambda energy: sum_start(0, 1, sum_end(0, 0, sums)))
    scalars = {}

    def finish_norm(energy):
        total = sum_rest(0, 1, more)
        scalars["norm"], scalars["energy"] = total[0:1], total[1:2]
        scalars["alpha"] = total[0:1] / total[1:2]

    def step_on(i, plane):
        end = slab(zed, i) + smoothed(image, 1, i, plane)
        put(res, i, slab(res, i) - scalars["alpha"] * slab(image, i))
        put(zed, i, slab(first, i) - scalars["alpha"] * end)

    def read_back(value_of, chosen):
        rows = []
        for i in chosen:
            value = jnp.where(odd_row, value_of(7 - i), value_of(i))
            for j in range(8):
                keep = (lane < 64) if j < 4 else (lane >= 64)
                rows.append(jnp.where(keep, value[j if j < 4 else 7 - j], 0.0))
        full = jnp.stack(rows).reshape(64 * len(chosen), 128)
        high = full.astype(jnp.bfloat16)
        low = (full - high.astype(F32)).astype(jnp.bfloat16)
        dims = (((1,), (1,)), ((), ()))
        return lax.dot_general(hot_both, high, dims, preferred_element_type=F32) + lax.dot_general(
            hot_both, low, dims, preferred_element_type=F32
        )

    def read_first():
        read[0] = read_back(lambda i: slab(first, i), range(8))

    apply_then(6, step_on, finish_norm, read_first)
    norm_0, energy_0, alpha_0 = scalars["norm"], scalars["energy"], scalars["alpha"]

    sums_of = {}

    def norm_and_cross(chosen):
        return (
            weighted(lambda i: slab(res, i), lambda i: slab(zed, i), chosen),
            weighted(lambda i: slab(zed, i), lambda i: slab(image, i), chosen),
        )

    def prepare():
        sums_of["norm"], sums_of["cross"] = norm_and_cross(range(1, 8))
        read[3] = read_back(lambda i: slab(image, i), range(8))

    energy, from_far, from_near = both_faces(7, prepare)
    norm, cross = norm_and_cross([0])
    norm, cross = norm + sums_of["norm"], cross + sums_of["cross"]
    more, cycle = forward_rest(7)
    energy = energy + more
    sums = sum_start(1, 0, stack_rows([norm, cross, energy]))
    assemble_own(7, 8, 24)
    read[1] = read_back(lambda i: slab(zed, i), range(8))
    totals = sum_end(1, 0, sums)
    for later in range(1, len(phases) - 1):
        totals = sum_end(1, later, sum_start(1, later, totals))
    sums = sum_start(1, len(phases) - 1, totals)
    read[2] = read_back(lambda i: slab(res, i), range(8))
    wait_all(cycle)
    middle = read_back(lambda i: whole_plane(7, i), range(2, 6))
    total = jnp.sum(sum_end(1, len(phases) - 1, sums), axis=1, keepdims=True)
    norm_1, cross_1, energy_1 = total[0:1], total[1:2], total[2:3]
    beta = norm_1 / norm_0
    alpha_1 = norm_1 / (energy_1 + 2.0 * beta * cross_1 + beta * beta * energy_0)
    solution_ref[...] = (alpha_0 + alpha_1 * beta) * read[0] + alpha_1 * read[1]
    residual = read[2] - (alpha_1 * beta) * read[3]
    residual_ref[:, 128:384] = residual[:, 128:384] - alpha_1 * middle
    wait_all(from_near)
    wait_all(from_far)
    ends = read_back(lambda i: whole_plane(7, i), (0, 1, 6, 7))
    residual_ref[:, 0:128] = residual[:, 0:128] - alpha_1 * ends[:, 0:128]
    residual_ref[:, 384:512] = residual[:, 384:512] - alpha_1 * ends[:, 128:256]
    for copy in started:
        copy.wait_send()


def solution(mesh):
    n_wide, n_narrow = mesh.shape["wide"], mesh.shape["narrow"]
    sides = 1 if n_narrow == 2 else 2
    factors = wide_factors(n_wide)
    partners = n_narrow * factors[0] - 1 + sum(factor - 1 for factor in factors[1:])
    vmem = pltpu.VMEM
    block = vmem((256, 128), F32)
    dma = pltpu.SemaphoreType.DMA

    def local(load, geom, element_order):
        whole = pl.BlockSpec(memory_space=pltpu.VMEM)
        shape = jax.ShapeDtypeStruct(load.shape, F32)
        return pl.pallas_call(
            functools.partial(body, n_wide, n_narrow),
            out_shape=(shape, shape),
            in_specs=[pl.BlockSpec(memory_space=pltpu.HBM)] * 3,
            out_specs=(whole, whole),
            scratch_shapes=[
                vmem(load.shape, F32),
                vmem(geom.shape, geom.dtype),
                vmem(element_order.shape, jnp.int32),
                vmem((7, 256, 128), F32),
                block,
                block,
                block,
                block,
                block,
                block,
                vmem((FIELDS, 256, 128), F32),
                vmem((FIELDS, sides, 64, 128), F32),
                vmem((FIELDS, 32, 128), F32),
                vmem((FIELDS, sides, 8, 128), F32),
                vmem((6, 32, 128), F32),
                vmem((6, 32, 128), F32),
                block,
                block,
                block,
                block,
                block,
                block,
                vmem((4, 64, 512), F32),
                vmem((2, len(factors), 8, 128), F32),
                vmem((FIELDS, 2, 32, 128), F32),
                vmem((FIELDS, sides, 64, 128), F32),
                vmem((FIELDS, sides, 2, 8, 128), F32),
                vmem((2, partners, 8, 128), F32),
                dma((FIELDS, 2)),
                dma((FIELDS, 2)),
                dma((FIELDS, sides)),
                dma((FIELDS, sides)),
                dma((FIELDS, sides, 2)),
                dma((FIELDS, sides, 2)),
                dma((2, partners)),
                dma((2, partners)),
                dma((3,)),
                dma((1,)),
                dma((1,)),
            ],
            compiler_params=pltpu.CompilerParams(
                collective_id=0, has_side_effects=True, vmem_limit_bytes=60 * 1024 * 1024
            ),
        )(load, geom, element_order)

    return jax.shard_map(
        local,
        mesh=mesh,
        in_specs=(
            P(("wide", "narrow"), None),
            P(None, ("wide", "narrow"), None),
            P("wide", "narrow", None),
        ),
        out_specs=(P(("wide", "narrow"), None), P(("wide", "narrow"), None)),
        check_vma=False,
    )
```
